512 devices in a mesh: grp: 16 (over y, x_hi), dev: 32 (over z, x_lo, core).
Axes of the slice: x: 4 (x_hi: 2, x_lo: 2; x = x_hi * 2 + x_lo), y: 8, z: 8, core: 2. Of those that a mesh axis runs over, the one named last changes fastest.
Arguments:
- velocities: bfloat16 [8192, 240, 512], P(('grp', 'dev')), may hold values from -6 to 6
- mass_root: float32 [240], replicated, may hold values from 1 to 4
- eigvec: float32 [2, 8, 240, 240], replicated, may hold values from -0.375 to 0.375
- q_points: int32 [3, 8], replicated, may hold values from 0 to 7
- cell_offsets: int32 [3, 512], replicated, may hold values from 0 to 7, as said below
Outputs:
- spectrum: float32 [16, 1920, 512], P('grp', 'dev')
The draws below stay inside these ranges and needn't reach their ends.
Inputs may be any that keep to these rules, and one draw needn't show every extreme that they name: `cell_offsets`: each cell of the 8 x 8 x 8 lattice appears exactly once.
All inputs are finite; a program needn't handle non-finite values.
Results may differ from the reference program's by a relative error of at most 0.0003.
Values sent between devices are 32-bit elements; how exact they have to be, the bound alone decides.
No kernel may reach another device: no remote copies, remote signals or barrier semaphores. Data moves between devices by JAX's collectives and lax.ppermute only.
A program may use at most 64 MiB of HBM per device.

```python
import math
import jax
import jax.numpy as jnp
from jax import lax

LAT = 8
CELLS = 512
DOF = 240
QPTS = 8
MODES = 1920
BLOCK = 512
TOTAL = 8192
N_GRP = 16


def draw_cell_offsets(key, part):
    key = jax.random.fold_in(key, 7)
    order = jax.random.permutation(key, CELLS).astype(jnp.int32)
    return jnp.stack([order // (LAT * LAT), order // LAT % LAT, order % LAT]).astype(jnp.int32)


def touch_ends(array, own_key, low, top_value):
    spot = [jax.random.randint(jax.random.fold_in(own_key, axis), (), 0, length) for axis, length in enumerate(array.shape)]
    main_axis = array.shape.index(max(array.shape))
    neighbour = spot[:main_axis] + [(spot[main_axis] + 1) % array.shape[main_axis]] + spot[main_axis + 1:]
    return array.at[tuple(spot)].set(low).at[tuple(neighbour)].set(top_value)


def block_scale(own_key, dims, shards, least, largest):
    level, own = 1.0, jax.random.fold_in(own_key, 6)
    for axis_at, parts in shards:
        steps = jnp.exp(jax.random.uniform(jax.random.fold_in(own, axis_at), (parts,), jnp.float32, least / len(shards), largest / len(shards)))
        level = level * jnp.repeat(steps, dims[axis_at] // parts).reshape([-1 if axis == axis_at else 1 for axis in range(len(dims))])
    return level


def normal_values(key, extent, scale, bound, split=(), dtype=jnp.bfloat16):
    gain = block_scale(key, extent, split, -0.22, 0.18) if split else 1.0
    array = jax.random.normal(key, extent, jnp.float32) * scale * gain
    return jnp.minimum(jnp.maximum(array, -bound), bound).astype(dtype)


def setup_inputs(seed: int = 0) -> dict:
    splits = jax.random.split(jax.random.key(seed), 6)
    velocities = normal_values(splits[0], (TOTAL, DOF, CELLS), 1.0, 6.0, ((0, 512),))
    mass_root = jnp.clip(jnp.exp(jax.random.uniform(splits[1], (DOF,), jnp.float32, math.log(1.0), math.log(4.0))), 1.0, 4.0)
    eigvec = normal_values(splits[2], (2, QPTS, DOF, DOF), DOF ** -0.5, 0.375, (), jnp.float32)
    q_points = touch_ends(jax.random.randint(splits[3], (3, QPTS), 0, LAT), jax.random.fold_in(splits[3], 1), 0, LAT - 1).astype(jnp.int32)
    cell_offsets = draw_cell_offsets(jax.random.fold_in(splits[5], 71), 0)
    return {"velocities": velocities, "mass_root": mass_root, "eigvec": eigvec, "q_points": q_points, "cell_offsets": cell_offsets}


def phase_table(q_points, cell_offsets, lattice, cells):
    products = jnp.sum(cell_offsets[:, :, None] * q_points[:, None, :], axis=0) % lattice
    angles = products.astype(jnp.float32) * (2.0 * math.pi / lattice)
    both = jnp.concatenate([jnp.cos(angles), jnp.sin(angles)], axis=1) * (cells ** -0.5)
    return both.astype(jnp.bfloat16)


def project_frames(frames_in, phases, mass_root, eigvec):
    nframes, ndof, ncells = frames_in.shape
    nqpts = phases.shape[1] // 2
    summed = jnp.dot(frames_in.reshape(nframes * ndof, ncells), phases, preferred_element_type=jnp.float32)
    summed = summed.reshape(nframes, ndof, 2, nqpts) * mass_root[None, :, None, None]
    real_s = summed[:, :, 0, :]
    imag_s = summed[:, :, 1, :]
    highest = lax.Precision.HIGHEST
    real_u = jnp.einsum('kbd,fdk->kbf', eigvec[0], real_s, precision=highest) + jnp.einsum('kbd,fdk->kbf', eigvec[1], imag_s, precision=highest)
    imag_u = jnp.einsum('kbd,fdk->kbf', eigvec[0], imag_s, precision=highest) - jnp.einsum('kbd,fdk->kbf', eigvec[1], real_s, precision=highest)
    return jnp.stack([real_u, imag_u]).reshape(2, nqpts * ndof, nframes)


def reference(velocities, mass_root, eigvec, q_points, cell_offsets):
    phases = phase_table(q_points, cell_offsets, LAT, CELLS)
    grouped = velocities.reshape(N_GRP, BLOCK, DOF, CELLS)
    series = lax.map(lambda frames_in: project_frames(frames_in, phases, mass_root, eigvec), grouped)
    series = jnp.moveaxis(series, 0, 2).reshape(2, MODES, TOTAL)
    spectra = jnp.fft.fft(series[0] + 1j * series[1], axis=-1)
    power = (jnp.real(spectra) ** 2 + jnp.imag(spectra) ** 2) / TOTAL
    return jnp.transpose(power.reshape(MODES, BLOCK, N_GRP), (2, 0, 1)).astype(jnp.float32)
```

```python
import functools
import math

import jax
import jax.numpy as jnp
import numpy as np
from jax import lax
from jax.experimental import pallas as pl
from jax.experimental.pallas import tpu as pltpu
from jax.sharding import PartitionSpec as P

LAT = 8
CELLS = 512
DOF = 240
QPTS = 8
TOTAL = 8192
N_GRP = 16
N_DEV = 32
FRAMES = 16
PER_DEV = 60
QUAD = 4
SPAN = 512
F32 = jnp.float32
BF16 = jnp.bfloat16


def split(x):
    hi = x.astype(BF16)
    return hi, (x - hi.astype(F32)).astype(BF16)


def dot_t(a, b):
    return lax.dot_general(a, b, (((1,), (1,)), ((), ())), preferred_element_type=F32)


def dot(a, b):
    return jnp.dot(a, b, preferred_element_type=F32)


def cosine_of(eighths):
    one = CELLS**-0.5
    half = math.sqrt(0.5) * CELLS**-0.5
    near = jnp.where((eighths == 1) | (eighths == 7), half, 0.0)
    far = jnp.where((eighths == 3) | (eighths == 5), -half, near)
    return jnp.where(eighths == 0, one, jnp.where(eighths == 4, -one, far))


def project_kernel(
    q_ref, cell_ref, mass_ref, vel_hbm, eig_hbm, out_ref, vel, eig, summed, series, vel_sem, eig_sem
):
    vel_copies = []
    for part in range(4):
        frames = pl.ds(part * 4, 4)
        copy = pltpu.make_async_copy(vel_hbm.at[frames], vel.at[frames], vel_sem.at[part])
        copy.start()
        vel_copies.append(copy)
    eig_copies = []
    for half in range(2):
        ks = pl.ds(half * 4, 4)
        for ri in range(2):
            copy = pltpu.make_async_copy(eig_hbm.at[ri, ks], eig.at[ri, ks], eig_sem.at[half * 2 + ri])
            copy.start()
            eig_copies.append(copy)

    row = lax.broadcasted_iota(jnp.int32, (QPTS, CELLS), 0)
    products = jnp.zeros((QPTS, CELLS), jnp.int32)
    for j in range(3):
        column = jnp.zeros((QPTS, CELLS), jnp.int32)
        for k in range(QPTS):
            column = jnp.where(row == k, q_ref[j, k], column)
        products = products + column * cell_ref[j : j + 1, :]
    eighths = products & (LAT - 1)
    phases = jnp.concatenate(
        [cosine_of(eighths), cosine_of((eighths + 6) & (LAT - 1))], axis=0
    ).astype(BF16)

    mass = mass_ref[...]
    for part in range(4):
        vel_copies[part].wait()
        for t in range(part * 4, part * 4 + 4):
            sums = dot_t(phases, vel[t]) * mass
            summed[0, t * 16 : (t + 1) * 16, :] = sums[:, :128]
            summed[1, t * 16 : (t + 1) * 16, : DOF - 128] = sums[:, 128:]

    series[1920:1928, :] = jnp.zeros((8, 128), F32)
    for half in range(2):
        first, second = [], []
        for kk in range(4):
            k = half * 4 + kk
            real, imag = [
                jnp.concatenate(
                    [summed[lanes, pl.ds(start, 16, stride=16), :] for lanes in range(2)], axis=1
                )[:, :DOF]
                for start in (k, 8 + k)
            ]
            first += [real, imag]
            second += [imag, -real]
        first = jnp.concatenate(split(jnp.concatenate(first, axis=0)), axis=0)
        second = jnp.concatenate(split(jnp.concatenate(second, axis=0)), axis=0)
        eig_copies[half * 2].wait()
        eig_copies[half * 2 + 1].wait()
        for kk in range(4):
            k = half * 4 + kk
            real_hi, real_lo = split(eig[0, k])
            imag_hi, imag_lo = split(eig[1, k])
            both = dot_t(real_hi, first) + dot_t(real_lo, first)
            both = both + dot_t(imag_hi, second) + dot_t(imag_lo, second)
            series[k * DOF : (k + 1) * DOF, :] = both[:, :128] + both[:, 128:]

    lane_quad = lax.broadcasted_iota(jnp.int32, (16, 128), 1) // 32
    for chunk in range(N_DEV):
        kk = chunk // 4 % 4
        message = None
        for i in range(QUAD):
            part = series[pl.ds(chunk * PER_DEV + i, 16, stride=QUAD), :]
            turn = (i - kk) * 32 % 128
            if turn:
                part = pltpu.roll(part, turn, 1)
            message = part if message is None else jnp.where(lane_quad == i, part, message)
        out_ref[chunk * 16 : (chunk + 1) * 16, :] = message


def project(velocities, mass_root, eigvec, q_points, cell_offsets):
    return pl.pallas_call(
        project_kernel,
        out_shape=jax.ShapeDtypeStruct((512, 128), F32),
        in_specs=[
            pl.BlockSpec(memory_space=pltpu.SMEM),
            pl.BlockSpec(memory_space=pltpu.VMEM),
            pl.BlockSpec(memory_space=pltpu.VMEM),
            pl.BlockSpec(memory_space=pl.ANY),
            pl.BlockSpec(memory_space=pl.ANY),
        ],
        out_specs=pl.BlockSpec(memory_space=pltpu.VMEM),
        scratch_shapes=[
            pltpu.VMEM((FRAMES, DOF, CELLS), BF16),
            pltpu.VMEM((2, QPTS, DOF, DOF), F32),
            pltpu.VMEM((2, 256, 128), F32),
            pltpu.VMEM((1928, 128), F32),
            pltpu.SemaphoreType.DMA((4,)),
            pltpu.SemaphoreType.DMA((4,)),
        ],
        compiler_params=pltpu.CompilerParams(vmem_limit_bytes=32 * 1024 * 1024),
        name="project",
    )(q_points, cell_offsets, mass_root.reshape(1, DOF), velocities, eigvec)


def transform_kernel(x_ref, low_ref, cos_ref, sin_ref, dft_ref, out_ref):
    lane = lax.broadcasted_iota(jnp.int32, (16, 128), 1)
    tiles = []
    for j in range(4):
        blocks = [x_ref[(8 * j + d) * 16 : (8 * j + d + 1) * 16, :] for d in range(8)]
        for bit in (4, 2, 1):
            width = bit * 16
            keep = (lane & width) == 0
            for a in range(8):
                if a & bit:
                    continue
                b = a | bit
                u, v = blocks[a], blocks[b]
                blocks[a] = jnp.where(keep, u, pltpu.roll(v, width, 1))
                blocks[b] = jnp.where(keep, pltpu.roll(u, 128 - width, 1), v)
        tiles.append(jnp.concatenate(blocks, axis=0))
    gathered = jnp.concatenate(tiles, axis=1)
    stacked = jnp.concatenate(split(gathered), axis=0)
    low = dot(low_ref[0], stacked) + dot(low_ref[1], stacked)
    real, imag = low[:64], low[64:]
    cosine, sine = cos_ref[...], sin_ref[...]
    turned = jnp.concatenate(
        [real * cosine + imag * sine, imag * cosine - real * sine], axis=0
    )
    hi, lo = split(turned)
    by_cos = dot(hi, dft_ref[0]) + dot(lo, dft_ref[0]) + dot(hi, dft_ref[2])
    by_sin = dot(hi, dft_ref[1]) + dot(lo, dft_ref[1]) + dot(hi, dft_ref[3])
    real = by_cos[:64] + by_sin[64:]
    imag = by_cos[64:] - by_sin[:64]
    power = (real * real + imag * imag) * (1.0 / TOTAL)
    for j in range(4):
        for i in range(QUAD):
            out_ref[pl.ds(j * 4 + i, 16, stride=16), :] = power[
                i * 16 : (i + 1) * 16, j * 128 : (j + 1) * 128
            ]


def split_np(x):
    hi = x.astype(np.float32).astype(jnp.bfloat16)
    lo = (x - hi.astype(np.float64)).astype(np.float32).astype(jnp.bfloat16)
    return hi, lo


@functools.cache
def tables():
    g = np.arange(16)
    theta = 2.0 * np.pi * (g[:, None] * g[None, :] % 16) / 16
    low = np.zeros((2, QUAD, 16, QUAD, 2, 16))
    for i in range(QUAD):
        low[0, i, :, i, 0] = np.cos(theta)
        low[0, i, :, i, 1] = np.sin(theta)
        low[1, i, :, i, 0] = -np.sin(theta)
        low[1, i, :, i, 1] = np.cos(theta)
    hi, lo = split_np(low.reshape(128, 128))
    low = np.stack([np.concatenate([hi, hi], axis=1), np.concatenate([lo, lo], axis=1)])
    s = np.arange(SPAN)
    twist = 2.0 * np.pi * np.tile(g[:, None] * s[None, :], (QUAD, 1)) / TOTAL
    full = 2.0 * np.pi * (s[:, None] * s[None, :] % SPAN) / SPAN
    cos_hi, cos_lo = split_np(np.cos(full))
    sin_hi, sin_lo = split_np(np.sin(full))
    dft = np.stack([cos_hi, sin_hi, cos_lo, sin_lo])
    return low, np.cos(twist).astype(np.float32), np.sin(twist).astype(np.float32), dft


def transform(x):
    return pl.pallas_call(
        transform_kernel,
        out_shape=jax.ShapeDtypeStruct((256, 128), F32),
        in_specs=[pl.BlockSpec(memory_space=pltpu.VMEM)] * 5,
        out_specs=pl.BlockSpec(memory_space=pltpu.VMEM),
        compiler_params=pltpu.CompilerParams(vmem_limit_bytes=32 * 1024 * 1024),
        name="transform",
    )(x, *[jnp.asarray(table) for table in tables()])


def order_kernel(x_ref, out_ref, rows):
    for j in range(4):
        for i in range(QUAD):
            rows[pl.ds(i, 16, stride=QUAD), :] = x_ref[pl.ds(j * 4 + i, 16, stride=16), :]
        out_ref[:, j * 128 : (j + 1) * 128] = rows[:PER_DEV, :]


def order(x):
    return pl.pallas_call(
        order_kernel,
        out_shape=jax.ShapeDtypeStruct((PER_DEV, SPAN), F32),
        in_specs=[pl.BlockSpec(memory_space=pltpu.VMEM)],
        out_specs=pl.BlockSpec(memory_space=pltpu.VMEM),
        scratch_shapes=[pltpu.VMEM((64, 128), F32)],
        name="order",
    )(x)


def per_device(velocities, mass_root, eigvec, q_points, cell_offsets):
    messages = project(velocities, mass_root, eigvec, q_points, cell_offsets)
    frames = lax.all_to_all(
        messages.reshape(512, 1, 128), ("dev", "grp"), 0, 0, tiled=True
    )
    power = transform(frames.reshape(512, 128))
    spectra = lax.all_to_all(power.reshape(16, 16, 128), "grp", 0, 0, tiled=True)
    return order(spectra.reshape(256, 128))[None]


def solution(mesh):
    return jax.shard_map(
        per_device,
        mesh=mesh,
        in_specs=(P(("grp", "dev"), None, None), P(), P(), P(), P()),
        out_specs=P("grp", "dev", None),
        check_vma=False,
    )
```

```python
import functools
import math

import jax
import jax.numpy as jnp
import numpy as np
from jax import lax
from jax.experimental import pallas as pl
from jax.experimental.pallas import tpu as pltpu
from jax.sharding import PartitionSpec as P

LAT = 8
CELLS = 512
DOF = 240
QPTS = 8
TOTAL = 8192
N_GRP = 16
N_DEV = 32
FRAMES = 16
PER_DEV = 60
QUAD = 4
SPAN = 512
F32 = jnp.float32
BF16 = jnp.bfloat16


def split(x):
    hi = x.astype(BF16)
    return hi, (x - hi.astype(F32)).astype(BF16)


def dot_t(a, b):
    return lax.dot_general(a, b, (((1,), (1,)), ((), ())), preferred_element_type=F32)


def dot(a, b):
    return jnp.dot(a, b, preferred_element_type=F32)


def cosine_of(eighths):
    one = CELLS**-0.5
    half = math.sqrt(0.5) * CELLS**-0.5
    near = jnp.where((eighths == 1) | (eighths == 7), half, 0.0)
    far = jnp.where((eighths == 3) | (eighths == 5), -half, near)
    return jnp.where(eighths == 0, one, jnp.where(eighths == 4, -one, far))


def project_kernel(
    q_hbm, cell_hbm, mass_hbm, vel_hbm, eig_hbm, out_ref,
    q_ref, cell_ref, mass_ref, vel, eig, summed, series, small_sem, vel_sem, eig_sem,
):
    small_copies = [
        pltpu.make_async_copy(source, target, small_sem.at[n])
        for n, (source, target) in enumerate(
            [(q_hbm, q_ref), (cell_hbm, cell_ref), (mass_hbm, mass_ref)]
        )
    ]
    for copy in small_copies:
        copy.start()
    vel_copies = []
    for part in range(4):
        frames = pl.ds(part * 4, 4)
        copy = pltpu.make_async_copy(vel_hbm.at[frames], vel.at[frames], vel_sem.at[part])
        copy.start()
        vel_copies.append(copy)
    eig_copies = []
    for half in range(2):
        ks = pl.ds(half * 4, 4)
        for ri in range(2):
            copy = pltpu.make_async_copy(eig_hbm.at[ri, ks], eig.at[ri, ks], eig_sem.at[half * 2 + ri])
            copy.start()
            eig_copies.append(copy)

    for copy in small_copies:
        copy.wait()
    row = lax.broadcasted_iota(jnp.int32, (QPTS, CELLS), 0)
    products = jnp.zeros((QPTS, CELLS), jnp.int32)
    for j in range(3):
        column = jnp.zeros((QPTS, CELLS), jnp.int32)
        for k in range(QPTS):
            column = jnp.where(row == k, q_ref[j, k], column)
        products = products + column * cell_ref[j : j + 1, :]
    eighths = products & (LAT - 1)
    phases = jnp.concatenate(
        [cosine_of(eighths), cosine_of((eighths + 6) & (LAT - 1))], axis=0
    ).astype(BF16)

    mass = mass_ref[...]
    for part in range(4):
        vel_copies[part].wait()
        for t in range(part * 4, part * 4 + 4):
            sums = dot_t(phases, vel[t]) * mass
            summed[0, t * 16 : (t + 1) * 16, :] = sums[:, :128]
            summed[1, t * 16 : (t + 1) * 16, : DOF - 128] = sums[:, 128:]

    series[1920:1928, :] = jnp.zeros((8, 128), F32)
    for half in range(2):
        first, second = [], []
        for kk in range(4):
            k = half * 4 + kk
            real, imag = [
                jnp.concatenate(
                    [summed[lanes, pl.ds(start, 16, stride=16), :] for lanes in range(2)], axis=1
                )[:, :DOF]
                for start in (k, 8 + k)
            ]
            first += [real, imag]
            second += [imag, -real]
        first = jnp.concatenate(split(jnp.concatenate(first, axis=0)), axis=0)
        second = jnp.concatenate(split(jnp.concatenate(second, axis=0)), axis=0)
        eig_copies[half * 2].wait()
        eig_copies[half * 2 + 1].wait()
        for kk in range(4):
            k = half * 4 + kk
            real_hi, real_lo = split(eig[0, k])
            imag_hi, imag_lo = split(eig[1, k])
            both = dot_t(real_hi, first) + dot_t(real_lo, first)
            both = both + dot_t(imag_hi, second) + dot_t(imag_lo, second)
            series[k * DOF : (k + 1) * DOF, :] = both[:, :128] + both[:, 128:]

    lane_quad = lax.broadcasted_iota(jnp.int32, (16, 128), 1) // 32
    for chunk in range(N_DEV):
        kk = chunk // 4 % 4
        message = None
        for i in range(QUAD):
            part = series[pl.ds(chunk * PER_DEV + i, 16, stride=QUAD), :]
            turn = (i - kk) * 32 % 128
            if turn:
                part = pltpu.roll(part, turn, 1)
            message = part if message is None else jnp.where(lane_quad == i, part, message)
        out_ref[chunk * 16 : (chunk + 1) * 16, :] = message


def project(velocities, mass_root, eigvec, q_points, cell_offsets):
    return pl.pallas_call(
        project_kernel,
        out_shape=jax.ShapeDtypeStruct((512, 128), F32),
        in_specs=[pl.BlockSpec(memory_space=pltpu.HBM)] * 5,
        out_specs=pl.BlockSpec(memory_space=pltpu.VMEM),
        scratch_shapes=[
            pltpu.SMEM((3, QPTS), jnp.int32),
            pltpu.VMEM((3, CELLS), jnp.int32),
            pltpu.VMEM((1, DOF), F32),
            pltpu.VMEM((FRAMES, DOF, CELLS), BF16),
            pltpu.VMEM((2, QPTS, DOF, DOF), F32),
            pltpu.VMEM((2, 256, 128), F32),
            pltpu.VMEM((1928, 128), F32),
            pltpu.SemaphoreType.DMA((3,)),
            pltpu.SemaphoreType.DMA((4,)),
            pltpu.SemaphoreType.DMA((4,)),
        ],
        compiler_params=pltpu.CompilerParams(vmem_limit_bytes=32 * 1024 * 1024),
        name="project",
    )(
        *[
            pltpu.with_memory_space_constraint(operand, pltpu.HBM)
            for operand in (q_points, cell_offsets, mass_root.reshape(1, DOF), velocities, eigvec)
        ]
    )


def transform_kernel(x_ref, low_ref, cos_ref, sin_ref, dft_ref, out_ref):
    lane = lax.broadcasted_iota(jnp.int32, (16, 128), 1)
    tiles = []
    for j in range(4):
        blocks = [x_ref[(8 * j + d) * 16 : (8 * j + d + 1) * 16, :] for d in range(8)]
        for bit in (4, 2, 1):
            width = bit * 16
            keep = (lane & width) == 0
            for a in range(8):
                if a & bit:
                    continue
                b = a | bit
                u, v = blocks[a], blocks[b]
                blocks[a] = jnp.where(keep, u, pltpu.roll(v, width, 1))
                blocks[b] = jnp.where(keep, pltpu.roll(u, 128 - width, 1), v)
        tiles.append(jnp.concatenate(blocks, axis=0))
    gathered = jnp.concatenate(tiles, axis=1)
    stacked = jnp.concatenate(split(gathered), axis=0)
    low = dot(low_ref[0], stacked) + dot(low_ref[1], stacked)
    real, imag = low[:64], low[64:]
    cosine, sine = cos_ref[...], sin_ref[...]
    turned = jnp.concatenate(
        [real * cosine + imag * sine, imag * cosine - real * sine], axis=0
    )
    hi, lo = split(turned)
    by_cos = dot(hi, dft_ref[0]) + dot(lo, dft_ref[0]) + dot(hi, dft_ref[2])
    by_sin = dot(hi, dft_ref[1]) + dot(lo, dft_ref[1]) + dot(hi, dft_ref[3])
    real = by_cos[:64] + by_sin[64:]
    imag = by_cos[64:] - by_sin[:64]
    power = (real * real + imag * imag) * (1.0 / TOTAL)
    for j in range(4):
        for i in range(QUAD):
            out_ref[pl.ds(i * 4 + j, 16, stride=16), :] = power[
                i * 16 : (i + 1) * 16, j * 128 : (j + 1) * 128
            ]


def split_np(x):
    hi = x.astype(np.float32).astype(jnp.bfloat16)
    lo = (x - hi.astype(np.float64)).astype(np.float32).astype(jnp.bfloat16)
    return hi, lo


@functools.cache
def tables():
    g = np.arange(16)
    theta = 2.0 * np.pi * (g[:, None] * g[None, :] % 16) / 16
    low = np.zeros((2, QUAD, 16, QUAD, 2, 16))
    for i in range(QUAD):
        low[0, i, :, i, 0] = np.cos(theta)
        low[0, i, :, i, 1] = np.sin(theta)
        low[1, i, :, i, 0] = -np.sin(theta)
        low[1, i, :, i, 1] = np.cos(theta)
    hi, lo = split_np(low.reshape(128, 128))
    low = np.stack([np.concatenate([hi, hi], axis=1), np.concatenate([lo, lo], axis=1)])
    s = np.arange(SPAN)
    twist = 2.0 * np.pi * np.tile(g[:, None] * s[None, :], (QUAD, 1)) / TOTAL
    full = 2.0 * np.pi * (s[:, None] * s[None, :] % SPAN) / SPAN
    cos_hi, cos_lo = split_np(np.cos(full))
    sin_hi, sin_lo = split_np(np.sin(full))
    dft = np.stack([cos_hi, sin_hi, cos_lo, sin_lo])
    return low, np.cos(twist).astype(np.float32), np.sin(twist).astype(np.float32), dft


def transform(x):
    return pl.pallas_call(
        transform_kernel,
        out_shape=jax.ShapeDtypeStruct((256, 128), F32),
        in_specs=[pl.BlockSpec(memory_space=pltpu.VMEM)] * 5,
        out_specs=pl.BlockSpec(memory_space=pltpu.VMEM),
        compiler_params=pltpu.CompilerParams(vmem_limit_bytes=32 * 1024 * 1024),
        name="transform",
    )(x, *[jnp.asarray(table) for table in tables()])


def per_device(velocities, mass_root, eigvec, q_points, cell_offsets):
    messages = project(velocities, mass_root, eigvec, q_points, cell_offsets)
    frames = lax.all_to_all(
        messages.reshape(512, 1, 128), ("dev", "grp"), 0, 0, tiled=True
    )
    power = transform(frames.reshape(512, 128))
    spectra = lax.all_to_all(power.reshape(16, 16, 128), "grp", 0, 0, tiled=True)
    rows = spectra.reshape(256, 128)[: PER_DEV * 4]
    return rows.reshape(1, PER_DEV, SPAN)


def solution(mesh):
    return jax.shard_map(
        per_device,
        mesh=mesh,
        in_specs=(P(("grp", "dev"), None, None), P(), P(), P(), P()),
        out_specs=P("grp", "dev", None),
        check_vma=False,
    )
```

```python
import functools
import math

import jax
import jax.numpy as jnp
import numpy as np
from jax import lax
from jax.experimental import pallas as pl
from jax.experimental.pallas import tpu as pltpu
from jax.sharding import Mesh
from jax.sharding import PartitionSpec as P

LAT = 8
CELLS = 512
DOF = 240
QPTS = 8
TOTAL = 8192
N_GRP = 16
N_DEV = 32
FRAMES = 16
PER_DEV = 60
QUAD = 4
SPAN = 512
GROUPS = np.arange(N_GRP).reshape(8, 2).T.ravel()
VEL_PARTS = 2
EIG_PARTS = ((0, 4), (4, 8))
EIG_STARTS = ((0,), (1,), ())
F32 = jnp.float32
BF16 = jnp.bfloat16


def split(x):
    hi = x.astype(BF16)
    return hi, (x - hi.astype(F32)).astype(BF16)


def dot_t(a, b):
    return lax.dot_general(a, b, (((1,), (1,)), ((), ())), preferred_element_type=F32)


def dot(a, b):
    return jnp.dot(a, b, preferred_element_type=F32)


def cosine_of(eighths):
    one = CELLS**-0.5
    half = math.sqrt(0.5) * CELLS**-0.5
    near = jnp.where((eighths == 1) | (eighths == 7), half, 0.0)
    far = jnp.where((eighths == 3) | (eighths == 5), -half, near)
    return jnp.where(eighths == 0, one, jnp.where(eighths == 4, -one, far))


def project_kernel(
    q_hbm, cell_hbm, mass_hbm, vel_hbm, eig_hbm, out_ref,
    q_ref, cell_ref, mass_ref, vel, eig, summed, series, small_sem, vel_sem, eig_sem,
):
    small_copies = [
        pltpu.make_async_copy(source, target, small_sem.at[n])
        for n, (source, target) in enumerate(
            [(q_hbm, q_ref), (cell_hbm, cell_ref), (mass_hbm, mass_ref)]
        )
    ]
    for copy in small_copies:
        copy.start()
    vel_copies = []
    for part in range(VEL_PARTS):
        frames = pl.ds(part * FRAMES // VEL_PARTS, FRAMES // VEL_PARTS)
        copy = pltpu.make_async_copy(vel_hbm.at[frames], vel.at[frames], vel_sem.at[part])
        copy.start()
        vel_copies.append(copy)
    eig_copies = []
    for part, (low, high) in enumerate(EIG_PARTS):
        ks = pl.ds(low, high - low)
        eig_copies.append(pltpu.make_async_copy(eig_hbm.at[:, ks], eig.at[:, ks], eig_sem.at[part]))
    for part in EIG_STARTS[0]:
        eig_copies[part].start()

    for copy in small_copies:
        copy.wait()
    row = lax.broadcasted_iota(jnp.int32, (QPTS, CELLS), 0)
    products = jnp.zeros((QPTS, CELLS), jnp.int32)
    for j in range(3):
        column = jnp.zeros((QPTS, CELLS), jnp.int32)
        for k in range(QPTS):
            column = jnp.where(row == k, q_ref[j, k], column)
        products = products + column * cell_ref[j : j + 1, :]
    eighths = products & (LAT - 1)
    phases = jnp.concatenate(
        [cosine_of(eighths), cosine_of((eighths + 6) & (LAT - 1))], axis=0
    ).astype(BF16)

    mass = mass_ref[...]
    for t in range(FRAMES):
        if t % (FRAMES // VEL_PARTS) == 0:
            vel_copies[t // (FRAMES // VEL_PARTS)].wait()
            for part in EIG_STARTS[1 + t // (FRAMES // VEL_PARTS)]:
                eig_copies[part].start()
        sums = dot_t(phases, vel[t]) * mass
        summed[0, t * 16 : (t + 1) * 16, :] = sums[:, :128]
        summed[1, t * 16 : (t + 1) * 16, : DOF - 128] = sums[:, 128:]

    series[:, DOF:, :] = jnp.zeros((QPTS, 8, 128), F32)
    lane_quad = lax.broadcasted_iota(jnp.int32, (16, 128), 1) // 32
    weights = []
    for k in range(QPTS):
        real, imag = [
            jnp.concatenate(
                [summed[lanes, pl.ds(start, 16, stride=16), :] for lanes in range(2)], axis=1
            )[:, :DOF]
            for start in (k, 8 + k)
        ]
        (real_hi, real_lo), (imag_hi, imag_lo) = split(real), split(imag)
        first = jnp.concatenate([real_hi, imag_hi] * 4 + [real_lo, imag_lo] * 4, axis=0)
        second = jnp.concatenate([imag_hi, -real_hi] * 4 + [imag_lo, -real_lo] * 4, axis=0)
        weights.append((first, second))
    for part, (low, high) in enumerate(EIG_PARTS):
        eig_copies[part].wait()
        for k in range(low, high):
            first, second = weights[k]
            real_hi, real_lo = split(eig[0, k])
            imag_hi, imag_lo = split(eig[1, k])
            both = dot_t(real_hi, first) + dot_t(real_lo, first)
            both = both + dot_t(imag_hi, second) + dot_t(imag_lo, second)
            series[k, :DOF, :] = both[:, :128] + both[:, 128:]
        for k in range(low, high):
            for chunk in range(4):
                message = None
                for i in range(QUAD):
                    rows = series[k, pl.ds(chunk * PER_DEV + i, 16, stride=QUAD), :]
                    message = rows if message is None else jnp.where(lane_quad == i, rows, message)
                out_ref[(4 * k + chunk) * 16 : (4 * k + chunk + 1) * 16, :] = message


def project(velocities, mass_root, eigvec, q_points, cell_offsets):
    return pl.pallas_call(
        project_kernel,
        out_shape=jax.ShapeDtypeStruct((512, 128), F32),
        in_specs=[pl.BlockSpec(memory_space=pltpu.HBM)] * 5,
        out_specs=pl.BlockSpec(memory_space=pltpu.VMEM),
        scratch_shapes=[
            pltpu.SMEM((3, QPTS), jnp.int32),
            pltpu.VMEM((3, CELLS), jnp.int32),
            pltpu.VMEM((1, DOF), F32),
            pltpu.VMEM((FRAMES, DOF, CELLS), BF16),
            pltpu.VMEM((2, QPTS, DOF, DOF), F32),
            pltpu.VMEM((2, 256, 128), F32),
            pltpu.VMEM((QPTS, DOF + 8, 128), F32),
            pltpu.SemaphoreType.DMA((3,)),
            pltpu.SemaphoreType.DMA((VEL_PARTS,)),
            pltpu.SemaphoreType.DMA((len(EIG_PARTS),)),
        ],
        compiler_params=pltpu.CompilerParams(vmem_limit_bytes=32 * 1024 * 1024),
        name="project",
    )(
        *[
            pltpu.with_memory_space_constraint(operand, pltpu.HBM)
            for operand in (q_points, cell_offsets, mass_root.reshape(1, DOF), velocities, eigvec)
        ]
    )


def transform_kernel(x_ref, low_ref, cos_ref, sin_ref, dft_ref, out_ref):
    lane = lax.broadcasted_iota(jnp.int32, (16, 128), 1)
    tiles = []
    for j in range(4):
        blocks = [x_ref[(8 * j + d) * 16 : (8 * j + d + 1) * 16, :] for d in range(8)]
        for bit in (4, 2, 1):
            width = bit * 16
            keep = (lane & width) == 0
            for a in range(8):
                if a & bit:
                    continue
                b = a | bit
                u, v = blocks[a], blocks[b]
                blocks[a] = jnp.where(keep, u, pltpu.roll(v, width, 1))
                blocks[b] = jnp.where(keep, pltpu.roll(u, 128 - width, 1), v)
        tiles.append(jnp.concatenate(blocks, axis=0))
    gathered = jnp.concatenate(tiles, axis=1)
    stacked = jnp.concatenate(split(gathered), axis=0)
    low = dot(low_ref[0], stacked) + dot(low_ref[1], stacked)
    real, imag = low[:64], low[64:]
    cosine, sine = cos_ref[...], sin_ref[...]
    turned = jnp.concatenate(
        [real * cosine + imag * sine, imag * cosine - real * sine], axis=0
    )
    hi, lo = split(turned)
    by_cos = dot(hi, dft_ref[0]) + dot(lo, dft_ref[0]) + dot(hi, dft_ref[2])
    by_sin = dot(hi, dft_ref[1]) + dot(lo, dft_ref[1]) + dot(hi, dft_ref[3])
    real = by_cos[:64] + by_sin[64:]
    imag = by_cos[64:] - by_sin[:64]
    power = (real * real + imag * imag) * (1.0 / TOTAL)
    for j in range(4):
        for i in range(QUAD):
            out_ref[pl.ds(i * 4 + j, 16, stride=16), :] = power[
                i * 16 : (i + 1) * 16, j * 128 : (j + 1) * 128
            ]


def split_np(x):
    hi = x.astype(np.float32).astype(jnp.bfloat16)
    lo = (x - hi.astype(np.float64)).astype(np.float32).astype(jnp.bfloat16)
    return hi, lo


@functools.cache
def tables():
    g = np.arange(16)
    theta = 2.0 * np.pi * (g[:, None] * g[None, :] % 16) / 16
    theta = theta[GROUPS][:, GROUPS]
    low = np.zeros((2, QUAD, 16, QUAD, 2, 16))
    for i in range(QUAD):
        low[0, i, :, i, 0] = np.cos(theta)
        low[0, i, :, i, 1] = np.sin(theta)
        low[1, i, :, i, 0] = -np.sin(theta)
        low[1, i, :, i, 1] = np.cos(theta)
    hi, lo = split_np(low.reshape(128, 128))
    low = np.stack([np.concatenate([hi, hi], axis=1), np.concatenate([lo, lo], axis=1)])
    s = np.arange(SPAN)
    twist = 2.0 * np.pi * np.tile(GROUPS[:, None] * s[None, :], (QUAD, 1)) / TOTAL
    full = 2.0 * np.pi * (s[:, None] * s[None, :] % SPAN) / SPAN
    cos_hi, cos_lo = split_np(np.cos(full))
    sin_hi, sin_lo = split_np(np.sin(full))
    dft = np.stack([cos_hi, sin_hi, cos_lo, sin_lo])
    return low, np.cos(twist).astype(np.float32), np.sin(twist).astype(np.float32), dft


def transform(x):
    return pl.pallas_call(
        transform_kernel,
        out_shape=jax.ShapeDtypeStruct((256, 128), F32),
        in_specs=[pl.BlockSpec(memory_space=pltpu.VMEM)] * 5,
        out_specs=pl.BlockSpec(memory_space=pltpu.VMEM),
        compiler_params=pltpu.CompilerParams(vmem_limit_bytes=32 * 1024 * 1024),
        name="transform",
    )(x, *[jnp.asarray(table) for table in tables()])


def per_device(velocities, mass_root, eigvec, q_points, cell_offsets):
    messages = project(velocities, mass_root, eigvec, q_points, cell_offsets)
    frames = lax.all_to_all(
        messages.reshape(512, 1, 128), ("dev", "grp_x", "grp_y"), 0, 0, tiled=True
    )
    power = transform(frames.reshape(512, 128))
    spectra = lax.all_to_all(
        power.reshape(16, 16, 128), ("grp_x", "grp_y"), 0, 0, tiled=True
    )
    rows = spectra.reshape(256, 128)[: PER_DEV * 4]
    return rows.reshape(1, PER_DEV, SPAN)


def solution(mesh):
    split_mesh = Mesh(mesh.devices.reshape(8, 2, N_DEV), ("grp_y", "grp_x", "dev"))
    grp = ("grp_y", "grp_x")
    return jax.shard_map(
        per_device,
        mesh=split_mesh,
        in_specs=(P(grp + ("dev",), None, None), P(), P(), P(), P()),
        out_specs=P(grp, "dev", None),
        check_vma=False,
    )
```

```python
import functools
import math

import jax
import jax.numpy as jnp
import numpy as np
from jax import lax
from jax.experimental import pallas as pl
from jax.experimental.pallas import tpu as pltpu
from jax.sharding import Mesh
from jax.sharding import PartitionSpec as P

LAT = 8
CELLS = 512
DOF = 240
QPTS = 8
TOTAL = 8192
N_GRP = 16
N_DEV = 32
FRAMES = 16
PER_DEV = 60
QUAD = 4
SPAN = 512
GROUPS = np.arange(N_GRP).reshape(8, 2).T.ravel()
VEL_PARTS = 2
EIG_PARTS = ((0, 4), (4, 8))
EIG_STARTS = ((0,), (1,), ())
F32 = jnp.float32
BF16 = jnp.bfloat16


def split(x):
    hi = x.astype(BF16)
    return hi, (x - hi.astype(F32)).astype(BF16)


def dot_t(a, b):
    return lax.dot_general(a, b, (((1,), (1,)), ((), ())), preferred_element_type=F32)


def dot(a, b):
    return jnp.dot(a, b, preferred_element_type=F32)


def cosine_of(eighths):
    one = CELLS**-0.5
    half = math.sqrt(0.5) * CELLS**-0.5
    near = jnp.where((eighths == 1) | (eighths == 7), half, 0.0)
    far = jnp.where((eighths == 3) | (eighths == 5), -half, near)
    return jnp.where(eighths == 0, one, jnp.where(eighths == 4, -one, far))


def project_kernel(
    q_hbm, cell_hbm, mass_hbm, vel_hbm, eig_hbm, out_ref,
    q_ref, cell_ref, mass_ref, vel, eig, summed, series, small_sem, vel_sem, eig_sem,
):
    small_copies = [
        pltpu.make_async_copy(source, target, small_sem.at[n])
        for n, (source, target) in enumerate(
            [(q_hbm, q_ref), (cell_hbm, cell_ref), (mass_hbm, mass_ref)]
        )
    ]
    for copy in small_copies:
        copy.start()
    vel_copies = []
    for part in range(VEL_PARTS):
        frames = pl.ds(part * FRAMES // VEL_PARTS, FRAMES // VEL_PARTS)
        copy = pltpu.make_async_copy(vel_hbm.at[frames], vel.at[frames], vel_sem.at[part])
        copy.start()
        vel_copies.append(copy)
    eig_copies = []
    for part, (low, high) in enumerate(EIG_PARTS):
        ks = pl.ds(low, high - low)
        eig_copies.append(pltpu.make_async_copy(eig_hbm.at[:, ks], eig.at[:, ks], eig_sem.at[part]))
    for part in EIG_STARTS[0]:
        eig_copies[part].start()

    for copy in small_copies:
        copy.wait()
    row = lax.broadcasted_iota(jnp.int32, (QPTS, CELLS), 0)
    products = jnp.zeros((QPTS, CELLS), jnp.int32)
    for j in range(3):
        column = jnp.zeros((QPTS, CELLS), jnp.int32)
        for k in range(QPTS):
            column = jnp.where(row == k, q_ref[j, k], column)
        products = products + column * cell_ref[j : j + 1, :]
    eighths = products & (LAT - 1)
    phases = jnp.concatenate(
        [cosine_of(eighths), cosine_of((eighths + 6) & (LAT - 1))], axis=0
    ).astype(BF16)

    mass = mass_ref[...]
    for t in range(FRAMES):
        if t % (FRAMES // VEL_PARTS) == 0:
            vel_copies[t // (FRAMES // VEL_PARTS)].wait()
            for part in EIG_STARTS[1 + t // (FRAMES // VEL_PARTS)]:
                eig_copies[part].start()
        sums = dot_t(phases, vel[t]) * mass
        at = (t % 2 * 8 + t // 2) * 16
        summed[0, at : at + 16, :] = sums[:, :128]
        summed[1, at : at + 16, : DOF - 128] = sums[:, 128:]

    series[:, DOF:, :] = jnp.zeros((QPTS, 8, 128), F32)
    lane_quad = lax.broadcasted_iota(jnp.int32, (16, 128), 1) // 32
    weights = []
    for k in range(QPTS):
        real, imag = [
            jnp.concatenate(
                [summed[lanes, pl.ds(start, 16, stride=16), :] for lanes in range(2)], axis=1
            )[:, :DOF]
            for start in (k, 8 + k)
        ]
        (real_hi, real_lo), (imag_hi, imag_lo) = split(real), split(imag)
        first = jnp.concatenate([real_hi, imag_hi] * 4 + [real_lo, imag_lo] * 4, axis=0)
        second = jnp.concatenate([imag_hi, -real_hi] * 4 + [imag_lo, -real_lo] * 4, axis=0)
        weights.append((first, second))
    for part, (low, high) in enumerate(EIG_PARTS):
        eig_copies[part].wait()
        for k in range(low, high):
            first, second = weights[k]
            real_hi, real_lo = split(eig[0, k])
            imag_hi, imag_lo = split(eig[1, k])
            both = dot_t(jnp.concatenate([real_hi, real_lo], axis=0), first)
            both = both + dot_t(jnp.concatenate([imag_hi, imag_lo], axis=0), second)
            series[k, :DOF, :] = (both[:DOF, :128] + both[:DOF, 128:]) + both[DOF:, :128]
        for k in range(low, high):
            for chunk in range(4):
                message = None
                for i in range(QUAD):
                    rows = series[k, pl.ds(chunk * PER_DEV + i, 16, stride=QUAD), :]
                    message = rows if message is None else jnp.where(lane_quad == i, rows, message)
                out_ref[(4 * k + chunk) * 16 : (4 * k + chunk + 1) * 16, :] = message


def project(velocities, mass_root, eigvec, q_points, cell_offsets):
    return pl.pallas_call(
        project_kernel,
        out_shape=jax.ShapeDtypeStruct((512, 128), F32),
        in_specs=[pl.BlockSpec(memory_space=pltpu.HBM)] * 5,
        out_specs=pl.BlockSpec(memory_space=pltpu.VMEM),
        scratch_shapes=[
            pltpu.SMEM((3, QPTS), jnp.int32),
            pltpu.VMEM((3, CELLS), jnp.int32),
            pltpu.VMEM((1, DOF), F32),
            pltpu.VMEM((FRAMES, DOF, CELLS), BF16),
            pltpu.VMEM((2, QPTS, DOF, DOF), F32),
            pltpu.VMEM((2, 256, 128), F32),
            pltpu.VMEM((QPTS, DOF + 8, 128), F32),
            pltpu.SemaphoreType.DMA((3,)),
            pltpu.SemaphoreType.DMA((VEL_PARTS,)),
            pltpu.SemaphoreType.DMA((len(EIG_PARTS),)),
        ],
        compiler_params=pltpu.CompilerParams(vmem_limit_bytes=32 * 1024 * 1024),
        name="project",
    )(
        *[
            pltpu.with_memory_space_constraint(operand, pltpu.HBM)
            for operand in (q_points, cell_offsets, mass_root.reshape(1, DOF), velocities, eigvec)
        ]
    )


def transform_kernel(x_ref, low_ref, twist_ref, dft_ref, turn_ref, out_ref):
    lane = lax.broadcasted_iota(jnp.int32, (16, 128), 1)
    tiles = []
    for j in range(2):
        blocks = [x_ref[(16 * j + d) * 16 : (16 * j + d + 1) * 16, :] for d in range(16)]
        for bit in (8, 4, 2, 1):
            width = bit * 8
            keep = (lane & width) == 0
            for a in range(16):
                if a & bit:
                    continue
                b = a | bit
                u, v = blocks[a], blocks[b]
                blocks[a] = jnp.where(keep, u, pltpu.roll(v, width, 1))
                blocks[b] = jnp.where(keep, pltpu.roll(u, 128 - width, 1), v)
        tiles.append(blocks)
    halves = []
    for parity in range(2):
        gathered = jnp.concatenate(
            [jnp.concatenate(blocks[parity::2], axis=0) for blocks in tiles], axis=1
        )
        stacked = jnp.concatenate(split(gathered), axis=0)
        low = dot(low_ref[0], stacked) + dot(low_ref[1], stacked)
        real, imag = low[:64], low[64:]
        cosine, sine = [
            jnp.concatenate([twist_ref[2 * parity + part]] * QUAD, axis=0) for part in range(2)
        ]
        halves += [real * cosine + imag * sine, imag * cosine - real * sine]
    hi, lo = split(jnp.concatenate(halves, axis=0))
    stacked = jnp.concatenate([hi, lo], axis=0)
    by_cos = dot(stacked, dft_ref[0])
    by_sin = dot(stacked, dft_ref[1])
    by_cos = by_cos[:256] + by_cos[256:] + dot(hi, dft_ref[2])
    by_sin = by_sin[:256] + by_sin[256:] + dot(hi, dft_ref[3])
    even_real = by_cos[:64] + by_sin[64:128]
    even_imag = by_cos[64:128] - by_sin[:64]
    real = by_cos[128:192] + by_sin[192:]
    imag = by_cos[192:] - by_sin[128:192]
    cosine, sine = turn_ref[0:1, :], turn_ref[1:2, :]
    odd_real = real * cosine + imag * sine
    odd_imag = imag * cosine - real * sine
    for half in range(2):
        if half:
            odd_real, odd_imag = -odd_real, -odd_imag
        real, imag = even_real + odd_real, even_imag + odd_imag
        power = (real * real + imag * imag) * (1.0 / TOTAL)
        for j in range(2):
            for i in range(QUAD):
                out_ref[pl.ds(i * 4 + half * 2 + j, 16, stride=16), :] = power[
                    i * 16 : (i + 1) * 16, j * 128 : (j + 1) * 128
                ]


def split_np(x):
    hi = x.astype(np.float32).astype(jnp.bfloat16)
    lo = (x - hi.astype(np.float64)).astype(np.float32).astype(jnp.bfloat16)
    return hi, lo


@functools.cache
def tables():
    g = np.arange(16)
    theta = 2.0 * np.pi * (g[:, None] * g[None, :] % 16) / 16
    theta = theta[GROUPS][:, GROUPS]
    low = np.zeros((2, QUAD, 16, QUAD, 2, 16))
    for i in range(QUAD):
        low[0, i, :, i, 0] = np.cos(theta)
        low[0, i, :, i, 1] = np.sin(theta)
        low[1, i, :, i, 0] = -np.sin(theta)
        low[1, i, :, i, 1] = np.cos(theta)
    hi, lo = split_np(low.reshape(128, 128))
    low = np.stack([np.concatenate([hi, hi], axis=1), np.concatenate([lo, lo], axis=1)])
    n = np.arange(SPAN // 2)
    s = np.stack([2 * n, 2 * n + 1])
    twist = 2.0 * np.pi * GROUPS[:, None] * s[:, None, :] / TOTAL
    twist = np.stack([np.cos(twist), np.sin(twist)], axis=1).reshape(4, 16, SPAN // 2)
    full = 2.0 * np.pi * (n[:, None] * n[None, :] % 256) / 256
    cos_hi, cos_lo = split_np(np.cos(full))
    sin_hi, sin_lo = split_np(np.sin(full))
    dft = np.stack([cos_hi, sin_hi, cos_lo, sin_lo])
    turn = 2.0 * np.pi * n / SPAN
    turn = np.stack([np.cos(turn), np.sin(turn)]).astype(np.float32)
    return low, twist.astype(np.float32), dft, turn


def transform(x):
    return pl.pallas_call(
        transform_kernel,
        out_shape=jax.ShapeDtypeStruct((256, 128), F32),
        in_specs=[pl.BlockSpec(memory_space=pltpu.VMEM)] * 5,
        out_specs=pl.BlockSpec(memory_space=pltpu.VMEM),
        compiler_params=pltpu.CompilerParams(vmem_limit_bytes=32 * 1024 * 1024),
        name="transform",
    )(x, *[jnp.asarray(table) for table in tables()])


def per_device(velocities, mass_root, eigvec, q_points, cell_offsets):
    messages = project(velocities, mass_root, eigvec, q_points, cell_offsets)
    frames = lax.all_to_all(
        messages.reshape(512, 1, 128), ("dev", "grp_x", "grp_y"), 0, 0, tiled=True
    )
    power = transform(frames.reshape(512, 128))
    spectra = lax.all_to_all(
        power.reshape(16, 16, 128), ("grp_x", "grp_y"), 0, 0, tiled=True
    )
    rows = spectra.reshape(256, 128)[: PER_DEV * 4]
    return rows.reshape(1, PER_DEV, SPAN)


def solution(mesh):
    split_mesh = Mesh(mesh.devices.reshape(8, 2, N_DEV), ("grp_y", "grp_x", "dev"))
    grp = ("grp_y", "grp_x")
    return jax.shard_map(
        per_device,
        mesh=split_mesh,
        in_specs=(P(grp + ("dev",), None, None), P(), P(), P(), P()),
        out_specs=P(grp, "dev", None),
        check_vma=False,
    )
```

```python
import functools
import math

import jax
import jax.numpy as jnp
import numpy as np
from jax import lax
from jax.experimental import pallas as pl
from jax.experimental.pallas import tpu as pltpu
from jax.sharding import Mesh
from jax.sharding import PartitionSpec as P

LAT = 8
CELLS = 512
DOF = 240
QPTS = 8
TOTAL = 8192
N_GRP = 16
N_DEV = 32
FRAMES = 16
PER_DEV = 60
QUAD = 4
SPAN = 512
GROUPS = np.arange(N_GRP).reshape(8, 2).T.ravel()
VEL_PARTS = 2
EIG_PARTS = ((0, 4), (4, 8))
EIG_STARTS = ((0,), (1,), ())
F32 = jnp.float32
BF16 = jnp.bfloat16


def split(x):
    hi = x.astype(BF16)
    return hi, (x - hi.astype(F32)).astype(BF16)


def dot_t(a, b):
    return lax.dot_general(a, b, (((1,), (1,)), ((), ())), preferred_element_type=F32)


def dot(a, b):
    return jnp.dot(a, b, preferred_element_type=F32)


def cosine_of(eighths):
    one = CELLS**-0.5
    half = math.sqrt(0.5) * CELLS**-0.5
    near = jnp.where((eighths == 1) | (eighths == 7), half, 0.0)
    far = jnp.where((eighths == 3) | (eighths == 5), -half, near)
    return jnp.where(eighths == 0, one, jnp.where(eighths == 4, -one, far))


def project_kernel(
    q_hbm, cell_hbm, mass_hbm, vel_hbm, eig_hbm, out_ref,
    q_ref, cell_ref, mass_ref, vel, eig, summed, series, small_sem, vel_sem, eig_sem,
):
    small_copies = [
        pltpu.make_async_copy(source, target, small_sem.at[n])
        for n, (source, target) in enumerate(
            [(q_hbm, q_ref), (cell_hbm, cell_ref), (mass_hbm, mass_ref)]
        )
    ]
    for copy in small_copies:
        copy.start()
    vel_copies = []
    for part in range(VEL_PARTS):
        frames = pl.ds(part * FRAMES // VEL_PARTS, FRAMES // VEL_PARTS)
        copy = pltpu.make_async_copy(vel_hbm.at[frames], vel.at[frames], vel_sem.at[part])
        copy.start()
        vel_copies.append(copy)
    eig_copies = []
    for part, (low, high) in enumerate(EIG_PARTS):
        ks = pl.ds(low, high - low)
        eig_copies.append(pltpu.make_async_copy(eig_hbm.at[:, ks], eig.at[:, ks], eig_sem.at[part]))
    for part in EIG_STARTS[0]:
        eig_copies[part].start()

    for copy in small_copies:
        copy.wait()
    row = lax.broadcasted_iota(jnp.int32, (QPTS, CELLS), 0)
    products = jnp.zeros((QPTS, CELLS), jnp.int32)
    for j in range(3):
        column = jnp.zeros((QPTS, CELLS), jnp.int32)
        for k in range(QPTS):
            column = jnp.where(row == k, q_ref[j, k], column)
        products = products + column * cell_ref[j : j + 1, :]
    eighths = products & (LAT - 1)
    phases = jnp.concatenate(
        [cosine_of(eighths), cosine_of((eighths + 6) & (LAT - 1))], axis=0
    ).astype(BF16)

    mass = mass_ref[...]
    for t in range(FRAMES):
        if t % (FRAMES // VEL_PARTS) == 0:
            vel_copies[t // (FRAMES // VEL_PARTS)].wait()
            for part in EIG_STARTS[1 + t // (FRAMES // VEL_PARTS)]:
                eig_copies[part].start()
        sums = dot_t(phases, vel[t]) * mass
        at = (t % 4 * 4 + t // 4) * 16
        summed[0, at : at + 16, :] = sums[:, :128]
        summed[1, at : at + 16, : DOF - 128] = sums[:, 128:]

    series[:, DOF:, :] = jnp.zeros((QPTS, 8, 128), F32)
    lane_quad = lax.broadcasted_iota(jnp.int32, (16, 128), 1) // 32
    weights = []
    for k in range(QPTS):
        real, imag = [
            jnp.concatenate(
                [summed[lanes, pl.ds(start, 16, stride=16), :] for lanes in range(2)], axis=1
            )[:, :DOF]
            for start in (k, 8 + k)
        ]
        (real_hi, real_lo), (imag_hi, imag_lo) = split(real), split(imag)
        first = jnp.concatenate([real_hi, imag_hi] * 4 + [real_lo, imag_lo] * 4, axis=0)
        second = jnp.concatenate([imag_hi, -real_hi] * 4 + [imag_lo, -real_lo] * 4, axis=0)
        weights.append((first, second))
    for part, (low, high) in enumerate(EIG_PARTS):
        eig_copies[part].wait()
        for k in range(low, high):
            first, second = weights[k]
            real_hi, real_lo = split(eig[0, k])
            imag_hi, imag_lo = split(eig[1, k])
            both = dot_t(jnp.concatenate([real_hi, real_lo], axis=0), first)
            both = both + dot_t(jnp.concatenate([imag_hi, imag_lo], axis=0), second)
            series[k, :DOF, :] = (both[:DOF, :128] + both[:DOF, 128:]) + both[DOF:, :128]
        for k in range(low, high):
            for chunk in range(4):
                message = None
                for i in range(QUAD):
                    rows = series[k, pl.ds(chunk * PER_DEV + i, 16, stride=QUAD), :]
                    message = rows if message is None else jnp.where(lane_quad == i, rows, message)
                out_ref[(4 * k + chunk) * 16 : (4 * k + chunk + 1) * 16, :] = message


def project(velocities, mass_root, eigvec, q_points, cell_offsets):
    return pl.pallas_call(
        project_kernel,
        out_shape=jax.ShapeDtypeStruct((512, 128), F32),
        in_specs=[pl.BlockSpec(memory_space=pltpu.HBM)] * 5,
        out_specs=pl.BlockSpec(memory_space=pltpu.VMEM),
        scratch_shapes=[
            pltpu.SMEM((3, QPTS), jnp.int32),
            pltpu.VMEM((3, CELLS), jnp.int32),
            pltpu.VMEM((1, DOF), F32),
            pltpu.VMEM((FRAMES, DOF, CELLS), BF16),
            pltpu.VMEM((2, QPTS, DOF, DOF), F32),
            pltpu.VMEM((2, 256, 128), F32),
            pltpu.VMEM((QPTS, DOF + 8, 128), F32),
            pltpu.SemaphoreType.DMA((3,)),
            pltpu.SemaphoreType.DMA((VEL_PARTS,)),
            pltpu.SemaphoreType.DMA((len(EIG_PARTS),)),
        ],
        compiler_params=pltpu.CompilerParams(vmem_limit_bytes=32 * 1024 * 1024),
        name="project",
    )(
        *[
            pltpu.with_memory_space_constraint(operand, pltpu.HBM)
            for operand in (q_points, cell_offsets, mass_root.reshape(1, DOF), velocities, eigvec)
        ]
    )


def transform_kernel(x_ref, low_ref, twist_ref, dft_ref, turn_ref, out_ref):
    block = lax.broadcasted_iota(jnp.int32, (16, 128), 1) // 4
    rows = [x_ref[d * 16 : (d + 1) * 16, :] for d in range(32)]
    rows = [pltpu.roll(row, 4 * d, 1) if d else row for d, row in enumerate(rows)]
    for bit in (1, 2, 4, 8, 16):
        moves = (block & bit) != 0
        rows = [jnp.where(moves, rows[(d + bit) % 32], rows[d]) for d in range(32)]
    rows = [rows[-n % 32] for n in range(32)]
    rows = [pltpu.roll(row, 128 - 4 * n, 1) if n else row for n, row in enumerate(rows)]
    parts = []
    for residue in range(4):
        gathered = jnp.concatenate(rows[residue::4], axis=0)
        stacked = jnp.concatenate(split(gathered), axis=0)
        low = dot(low_ref[0], stacked) + dot(low_ref[1], stacked)
        real, imag = low[:64], low[64:]
        cosine, sine = [
            jnp.concatenate([twist_ref[2 * residue + part]] * QUAD, axis=0) for part in range(2)
        ]
        parts += [real * cosine + imag * sine, imag * cosine - real * sine]
    both = jnp.concatenate(split(jnp.concatenate(parts, axis=0)), axis=1)
    both = dot(both, dft_ref[0]) + dot(both, dft_ref[1])
    real, imag = [], []
    for residue in range(4):
        upper = both[residue * 128 : residue * 128 + 64]
        lower = both[residue * 128 + 64 : residue * 128 + 128]
        a = upper[:, :128] + lower[:, 128:]
        b = lower[:, :128] - upper[:, 128:]
        if residue:
            cosine = turn_ref[2 * residue : 2 * residue + 1, :]
            sine = turn_ref[2 * residue + 1 : 2 * residue + 2, :]
            a, b = a * cosine + b * sine, b * cosine - a * sine
        real.append(a)
        imag.append(b)
    sum_real, sum_imag = real[0] + real[2], imag[0] + imag[2]
    gap_real, gap_imag = real[0] - real[2], imag[0] - imag[2]
    odd_real, odd_imag = real[1] + real[3], imag[1] + imag[3]
    far_real, far_imag = real[1] - real[3], imag[1] - imag[3]
    quarters = [
        (sum_real + odd_real, sum_imag + odd_imag),
        (gap_real + far_imag, gap_imag - far_real),
        (sum_real - odd_real, sum_imag - odd_imag),
        (gap_real - far_imag, gap_imag + far_real),
    ]
    for j, (a, b) in enumerate(quarters):
        power = (a * a + b * b) * (1.0 / TOTAL)
        for i in range(QUAD):
            out_ref[pl.ds(i * 4 + j, 16, stride=16), :] = power[i * 16 : (i + 1) * 16, :]


def split_np(x):
    hi = x.astype(np.float32).astype(jnp.bfloat16)
    lo = (x - hi.astype(np.float64)).astype(np.float32).astype(jnp.bfloat16)
    return hi, lo


@functools.cache
def tables():
    g = np.arange(16)
    theta = 2.0 * np.pi * (g[:, None] * g[None, :] % 16) / 16
    theta = theta[GROUPS][:, GROUPS]
    low = np.zeros((2, QUAD, 16, QUAD, 2, 16))
    for i in range(QUAD):
        low[0, i, :, i, 0] = np.cos(theta)
        low[0, i, :, i, 1] = np.sin(theta)
        low[1, i, :, i, 0] = -np.sin(theta)
        low[1, i, :, i, 1] = np.cos(theta)
    hi, lo = split_np(low.reshape(128, 128))
    low = np.stack([np.concatenate([hi, hi], axis=1), np.concatenate([lo, lo], axis=1)])
    n = np.arange(SPAN // 4)
    residue = np.arange(4)
    s = 4 * n[None, :] + residue[:, None]
    twist = 2.0 * np.pi * GROUPS[:, None] * s[:, None, :] / TOTAL
    twist = np.stack([np.cos(twist), np.sin(twist)], axis=1).reshape(8, 16, SPAN // 4)
    full = 2.0 * np.pi * (n[:, None] * n[None, :] % 128) / 128
    hi, lo = split_np(np.concatenate([np.cos(full), np.sin(full)], axis=1))
    dft = np.stack([np.concatenate([hi, hi], axis=0), np.concatenate([lo, np.zeros_like(lo)], axis=0)])
    turn = 2.0 * np.pi * residue[:, None] * n / SPAN
    turn = np.stack([np.cos(turn), np.sin(turn)], axis=1).reshape(8, SPAN // 4)
    return low, twist.astype(np.float32), dft, turn.astype(np.float32)


def transform(x):
    return pl.pallas_call(
        transform_kernel,
        out_shape=jax.ShapeDtypeStruct((256, 128), F32),
        in_specs=[pl.BlockSpec(memory_space=pltpu.VMEM)] * 5,
        out_specs=pl.BlockSpec(memory_space=pltpu.VMEM),
        compiler_params=pltpu.CompilerParams(vmem_limit_bytes=32 * 1024 * 1024),
        name="transform",
    )(x, *[jnp.asarray(table) for table in tables()])


def per_device(velocities, mass_root, eigvec, q_points, cell_offsets):
    messages = project(velocities, mass_root, eigvec, q_points, cell_offsets)
    frames = lax.all_to_all(
        messages.reshape(512, 1, 128), ("dev", "grp_x", "grp_y"), 0, 0, tiled=True
    )
    power = transform(frames.reshape(512, 128))
    spectra = lax.all_to_all(
        power.reshape(16, 16, 128), ("grp_x", "grp_y"), 0, 0, tiled=True
    )
    rows = spectra.reshape(256, 128)[: PER_DEV * 4]
    return rows.reshape(1, PER_DEV, SPAN)


def solution(mesh):
    split_mesh = Mesh(mesh.devices.reshape(8, 2, N_DEV), ("grp_y", "grp_x", "dev"))
    grp = ("grp_y", "grp_x")
    return jax.shard_map(
        per_device,
        mesh=split_mesh,
        in_specs=(P(grp + ("dev",), None, None), P(), P(), P(), P()),
        out_specs=P(grp, "dev", None),
        check_vma=False,
    )
```

```python
import functools
import math

import jax
import jax.numpy as jnp
import numpy as np
from jax import lax
from jax.experimental import pallas as pl
from jax.experimental.pallas import tpu as pltpu
from jax.sharding import Mesh
from jax.sharding import PartitionSpec as P

LAT = 8
CELLS = 512
DOF = 240
QPTS = 8
TOTAL = 8192
N_GRP = 16
N_DEV = 32
FRAMES = 16
PER_DEV = 60
QUAD = 4
SPAN = 512
GROUPS = np.arange(N_GRP).reshape(8, 2).T.ravel()
VEL_PARTS = 2
EIG_PARTS = ((0, 4), (4, 8))
EIG_STARTS = ((0,), (1,), ())
F32 = jnp.float32
BF16 = jnp.bfloat16


def split(x):
    hi = x.astype(BF16)
    return hi, (x - hi.astype(F32)).astype(BF16)


def dot_t(a, b):
    return lax.dot_general(a, b, (((1,), (1,)), ((), ())), preferred_element_type=F32)


def dot(a, b):
    return jnp.dot(a, b, preferred_element_type=F32)


def cosine_of(eighths):
    one = CELLS**-0.5
    half = math.sqrt(0.5) * CELLS**-0.5
    near = jnp.where((eighths == 1) | (eighths == 7), half, 0.0)
    far = jnp.where((eighths == 3) | (eighths == 5), -half, near)
    return jnp.where(eighths == 0, one, jnp.where(eighths == 4, -one, far))


def project_kernel(
    q_hbm, cell_hbm, mass_hbm, vel_hbm, eig_hbm, out_ref,
    q_ref, cell_ref, mass_ref, vel, eig, summed, series, small_sem, vel_sem, eig_sem,
):
    small_copies = [
        pltpu.make_async_copy(source, target, small_sem.at[n])
        for n, (source, target) in enumerate(
            [(q_hbm, q_ref), (cell_hbm, cell_ref), (mass_hbm, mass_ref)]
        )
    ]
    for copy in small_copies:
        copy.start()
    vel_copies = []
    for part in range(VEL_PARTS):
        frames = pl.ds(part * FRAMES // VEL_PARTS, FRAMES // VEL_PARTS)
        copy = pltpu.make_async_copy(vel_hbm.at[frames], vel.at[frames], vel_sem.at[part])
        copy.start()
        vel_copies.append(copy)
    eig_copies = []
    for part, (low, high) in enumerate(EIG_PARTS):
        ks = pl.ds(low, high - low)
        eig_copies.append(pltpu.make_async_copy(eig_hbm.at[:, ks], eig.at[:, ks], eig_sem.at[part]))
    for part in EIG_STARTS[0]:
        eig_copies[part].start()

    for copy in small_copies:
        copy.wait()
    row = lax.broadcasted_iota(jnp.int32, (QPTS, CELLS), 0)
    products = jnp.zeros((QPTS, CELLS), jnp.int32)
    for j in range(3):
        column = jnp.zeros((QPTS, CELLS), jnp.int32)
        for k in range(QPTS):
            column = jnp.where(row == k, q_ref[j, k], column)
        products = products + column * cell_ref[j : j + 1, :]
    eighths = products & (LAT - 1)
    phases = jnp.concatenate(
        [cosine_of(eighths), cosine_of((eighths + 6) & (LAT - 1))], axis=0
    ).astype(BF16)

    mass = mass_ref[...]
    for t in range(FRAMES):
        if t % (FRAMES // VEL_PARTS) == 0:
            vel_copies[t // (FRAMES // VEL_PARTS)].wait()
            for part in EIG_STARTS[1 + t // (FRAMES // VEL_PARTS)]:
                eig_copies[part].start()
        sums = dot_t(phases, vel[t]) * mass
        at = (t % 4 * 4 + t // 4) * 16
        summed[0, at : at + 16, :] = sums[:, :128]
        summed[1, at : at + 16, : DOF - 128] = sums[:, 128:]

    series[:, DOF:, :] = jnp.zeros((QPTS, 8, 128), F32)
    lane_quad = lax.broadcasted_iota(jnp.int32, (16, 128), 1) // 32
    weights = []
    for k in range(QPTS):
        real, imag = [
            jnp.concatenate(
                [summed[lanes, pl.ds(start, 16, stride=16), :] for lanes in range(2)], axis=1
            )[:, :DOF]
            for start in (k, 8 + k)
        ]
        (real_hi, real_lo), (imag_hi, imag_lo) = split(real), split(imag)
        first = jnp.concatenate([real_hi, imag_hi] * 4 + [real_lo, imag_lo] * 4, axis=0)
        second = jnp.concatenate([imag_hi, -real_hi] * 4 + [imag_lo, -real_lo] * 4, axis=0)
        weights.append((first, second))
    for part, (low, high) in enumerate(EIG_PARTS):
        eig_copies[part].wait()
        for k in range(low, high):
            first, second = weights[k]
            real_hi, real_lo = split(eig[0, k])
            imag_hi, imag_lo = split(eig[1, k])
            both = dot_t(jnp.concatenate([real_hi, real_lo], axis=0), first)
            both = both + dot_t(jnp.concatenate([imag_hi, imag_lo], axis=0), second)
            series[k, :DOF, :] = (both[:DOF, :128] + both[:DOF, 128:]) + both[DOF:, :128]
        for k in range(low, high):
            for chunk in range(4):
                message = None
                for i in range(QUAD):
                    rows = series[k, pl.ds(chunk * PER_DEV + i, 16, stride=QUAD), :]
                    message = rows if message is None else jnp.where(lane_quad == i, rows, message)
                out_ref[(4 * k + chunk) * 16 : (4 * k + chunk + 1) * 16, :] = message


def project(velocities, mass_root, eigvec, q_points, cell_offsets):
    return pl.pallas_call(
        project_kernel,
        out_shape=jax.ShapeDtypeStruct((512, 128), F32),
        in_specs=[pl.BlockSpec(memory_space=pltpu.HBM)] * 5,
        out_specs=pl.BlockSpec(memory_space=pltpu.VMEM),
        scratch_shapes=[
            pltpu.SMEM((3, QPTS), jnp.int32),
            pltpu.VMEM((3, CELLS), jnp.int32),
            pltpu.VMEM((1, DOF), F32),
            pltpu.VMEM((FRAMES, DOF, CELLS), BF16),
            pltpu.VMEM((2, QPTS, DOF, DOF), F32),
            pltpu.VMEM((2, 256, 128), F32),
            pltpu.VMEM((QPTS, DOF + 8, 128), F32),
            pltpu.SemaphoreType.DMA((3,)),
            pltpu.SemaphoreType.DMA((VEL_PARTS,)),
            pltpu.SemaphoreType.DMA((len(EIG_PARTS),)),
        ],
        compiler_params=pltpu.CompilerParams(vmem_limit_bytes=32 * 1024 * 1024),
        name="project",
    )(
        *[
            pltpu.with_memory_space_constraint(operand, pltpu.HBM)
            for operand in (q_points, cell_offsets, mass_root.reshape(1, DOF), velocities, eigvec)
        ]
    )


def transform_kernel(x_ref, low_ref, twist_ref, dft_ref, turn_ref, out_ref):
    block = lax.broadcasted_iota(jnp.int32, (16, 128), 1) // 4
    rows = [x_ref[d * 16 : (d + 1) * 16, :] for d in range(32)]
    rows = [pltpu.roll(row, 4 * d, 1) if d else row for d, row in enumerate(rows)]
    for bit in (1, 2, 4, 8, 16):
        moves = (block & bit) != 0
        rows = [jnp.where(moves, rows[(d + bit) % 32], rows[d]) for d in range(32)]
    rows = [rows[-n % 32] for n in range(32)]
    rows = [pltpu.roll(row, 128 - 4 * n, 1) if n else row for n, row in enumerate(rows)]
    low_hi = jnp.concatenate([low_ref[0]] * 2, axis=1)
    parts = []
    for residue in range(4):
        gathered = jnp.concatenate(rows[residue::4], axis=0)
        hi, lo = split(gathered)
        low = dot(low_hi, jnp.concatenate([hi, lo], axis=0)) + dot(low_ref[1], hi)
        real, imag = low[:64], low[64:]
        cosine, sine = [
            jnp.concatenate([twist_ref[2 * residue + part]] * QUAD, axis=0) for part in range(2)
        ]
        parts += [real * cosine + imag * sine, imag * cosine - real * sine]
    hi, lo = split(jnp.concatenate(parts, axis=0))
    both = dot(jnp.concatenate([hi, lo], axis=1), jnp.concatenate([dft_ref[0]] * 2, axis=0))
    both = both + dot(hi, dft_ref[1])
    real, imag = [], []
    for residue in range(4):
        upper = both[residue * 128 : residue * 128 + 64]
        lower = both[residue * 128 + 64 : residue * 128 + 128]
        a = upper[:, :128] + lower[:, 128:]
        b = lower[:, :128] - upper[:, 128:]
        if residue:
            cosine = turn_ref[2 * residue : 2 * residue + 1, :]
            sine = turn_ref[2 * residue + 1 : 2 * residue + 2, :]
            a, b = a * cosine + b * sine, b * cosine - a * sine
        real.append(a)
        imag.append(b)
    sum_real, sum_imag = real[0] + real[2], imag[0] + imag[2]
    gap_real, gap_imag = real[0] - real[2], imag[0] - imag[2]
    odd_real, odd_imag = real[1] + real[3], imag[1] + imag[3]
    far_real, far_imag = real[1] - real[3], imag[1] - imag[3]
    quarters = [
        (sum_real + odd_real, sum_imag + odd_imag),
        (gap_real + far_imag, gap_imag - far_real),
        (sum_real - odd_real, sum_imag - odd_imag),
        (gap_real - far_imag, gap_imag + far_real),
    ]
    for j, (a, b) in enumerate(quarters):
        power = (a * a + b * b) * (1.0 / TOTAL)
        for i in range(QUAD):
            out_ref[pl.ds(i * 4 + j, 16, stride=16), :] = power[i * 16 : (i + 1) * 16, :]


def split_np(x):
    hi = x.astype(np.float32).astype(jnp.bfloat16)
    lo = (x - hi.astype(np.float64)).astype(np.float32).astype(jnp.bfloat16)
    return hi, lo


@functools.cache
def tables():
    g = np.arange(16)
    theta = 2.0 * np.pi * (g[:, None] * g[None, :] % 16) / 16
    theta = theta[GROUPS][:, GROUPS]
    low = np.zeros((2, QUAD, 16, QUAD, 2, 16))
    for i in range(QUAD):
        low[0, i, :, i, 0] = np.cos(theta)
        low[0, i, :, i, 1] = np.sin(theta)
        low[1, i, :, i, 0] = -np.sin(theta)
        low[1, i, :, i, 1] = np.cos(theta)
    hi, lo = split_np(low.reshape(128, 128))
    low = np.stack([hi, lo])
    n = np.arange(SPAN // 4)
    residue = np.arange(4)
    s = 4 * n[None, :] + residue[:, None]
    twist = 2.0 * np.pi * GROUPS[:, None] * s[:, None, :] / TOTAL
    twist = np.stack([np.cos(twist), np.sin(twist)], axis=1).reshape(8, 16, SPAN // 4)
    full = 2.0 * np.pi * (n[:, None] * n[None, :] % 128) / 128
    hi, lo = split_np(np.concatenate([np.cos(full), np.sin(full)], axis=1))
    dft = np.stack([hi, lo])
    turn = 2.0 * np.pi * residue[:, None] * n / SPAN
    turn = np.stack([np.cos(turn), np.sin(turn)], axis=1).reshape(8, SPAN // 4)
    return low, twist.astype(np.float32), dft, turn.astype(np.float32)


def transform(x):
    return pl.pallas_call(
        transform_kernel,
        out_shape=jax.ShapeDtypeStruct((256, 128), F32),
        in_specs=[pl.BlockSpec(memory_space=pltpu.VMEM)] * 5,
        out_specs=pl.BlockSpec(memory_space=pltpu.VMEM),
        compiler_params=pltpu.CompilerParams(vmem_limit_bytes=32 * 1024 * 1024),
        name="transform",
    )(x, *[jnp.asarray(table) for table in tables()])


def per_device(velocities, mass_root, eigvec, q_points, cell_offsets):
    messages = project(velocities, mass_root, eigvec, q_points, cell_offsets)
    frames = lax.all_to_all(
        messages.reshape(512, 1, 128), ("dev", "grp_x", "grp_y"), 0, 0, tiled=True
    )
    power = transform(frames.reshape(512, 128))
    spectra = lax.all_to_all(
        power.reshape(16, 16, 128), ("grp_x", "grp_y"), 0, 0, tiled=True
    )
    rows = spectra.reshape(256, 128)[: PER_DEV * 4]
    return rows.reshape(1, PER_DEV, SPAN)


def solution(mesh):
    split_mesh = Mesh(mesh.devices.reshape(8, 2, N_DEV), ("grp_y", "grp_x", "dev"))
    grp = ("grp_y", "grp_x")
    return jax.shard_map(
        per_device,
        mesh=split_mesh,
        in_specs=(P(grp + ("dev",), None, None), P(), P(), P(), P()),
        out_specs=P(grp, "dev", None),
        check_vma=False,
    )
```

```python
import functools
import math

import jax
import jax.numpy as jnp
import numpy as np
from jax import lax
from jax.experimental import pallas as pl
from jax.experimental.pallas import tpu as pltpu
from jax.sharding import Mesh
from jax.sharding import PartitionSpec as P

LAT = 8
CELLS = 512
DOF = 240
QPTS = 8
TOTAL = 8192
N_GRP = 16
N_DEV = 32
FRAMES = 16
PER_DEV = 60
QUAD = 4
SPAN = 512
GROUPS = np.arange(N_GRP).reshape(2, 4, 2).transpose(0, 2, 1).ravel()
VEL_PARTS = 2
EIG_PARTS = ((0, 4), (4, 8))
EIG_STARTS = ((0,), (1,), ())
F32 = jnp.float32
BF16 = jnp.bfloat16


def split(x):
    hi = x.astype(BF16)
    return hi, (x - hi.astype(F32)).astype(BF16)


def dot_t(a, b):
    return lax.dot_general(a, b, (((1,), (1,)), ((), ())), preferred_element_type=F32)


def dot(a, b):
    return jnp.dot(a, b, preferred_element_type=F32)


def cosine_of(eighths):
    one = CELLS**-0.5
    half = math.sqrt(0.5) * CELLS**-0.5
    near = jnp.where((eighths == 1) | (eighths == 7), half, 0.0)
    far = jnp.where((eighths == 3) | (eighths == 5), -half, near)
    return jnp.where(eighths == 0, one, jnp.where(eighths == 4, -one, far))


def project_kernel(
    q_hbm, cell_hbm, mass_hbm, vel_hbm, eig_hbm, out_ref,
    q_ref, cell_ref, mass_ref, vel, eig, summed, series, small_sem, vel_sem, eig_sem,
):
    small_copies = [
        pltpu.make_async_copy(source, target, small_sem.at[n])
        for n, (source, target) in enumerate(
            [(q_hbm, q_ref), (cell_hbm, cell_ref), (mass_hbm, mass_ref)]
        )
    ]
    for copy in small_copies:
        copy.start()
    vel_copies = []
    for part in range(VEL_PARTS):
        frames = pl.ds(part * FRAMES // VEL_PARTS, FRAMES // VEL_PARTS)
        copy = pltpu.make_async_copy(vel_hbm.at[frames], vel.at[frames], vel_sem.at[part])
        copy.start()
        vel_copies.append(copy)
    eig_copies = []
    for part, (low, high) in enumerate(EIG_PARTS):
        ks = pl.ds(low, high - low)
        eig_copies.append(pltpu.make_async_copy(eig_hbm.at[:, ks], eig.at[:, ks], eig_sem.at[part]))
    for part in EIG_STARTS[0]:
        eig_copies[part].start()

    for copy in small_copies:
        copy.wait()
    row = lax.broadcasted_iota(jnp.int32, (QPTS, CELLS), 0)
    products = jnp.zeros((QPTS, CELLS), jnp.int32)
    for j in range(3):
        column = jnp.zeros((QPTS, CELLS), jnp.int32)
        for k in range(QPTS):
            column = jnp.where(row == k, q_ref[j, k], column)
        products = products + column * cell_ref[j : j + 1, :]
    eighths = products & (LAT - 1)
    phases = jnp.concatenate(
        [cosine_of(eighths), cosine_of((eighths + 6) & (LAT - 1))], axis=0
    ).astype(BF16)

    mass = mass_ref[...]
    for t in range(FRAMES):
        if t % (FRAMES // VEL_PARTS) == 0:
            vel_copies[t // (FRAMES // VEL_PARTS)].wait()
            for part in EIG_STARTS[1 + t // (FRAMES // VEL_PARTS)]:
                eig_copies[part].start()
        sums = dot_t(phases, vel[t]) * mass
        at = (t % 4 * 4 + t // 4) * 16
        summed[0, at : at + 16, :] = sums[:, :128]
        summed[1, at : at + 16, : DOF - 128] = sums[:, 128:]

    series[:, DOF:, :] = jnp.zeros((QPTS, 8, 128), F32)
    lane_quad = lax.broadcasted_iota(jnp.int32, (16, 128), 1) // 32
    weights = []
    for k in range(QPTS):
        real, imag = [
            jnp.concatenate(
                [summed[lanes, pl.ds(start, 16, stride=16), :] for lanes in range(2)], axis=1
            )[:, :DOF]
            for start in (k, 8 + k)
        ]
        (real_hi, real_lo), (imag_hi, imag_lo) = split(real), split(imag)
        first = jnp.concatenate([real_hi, imag_hi] * 4 + [real_lo, imag_lo] * 4, axis=0)
        second = jnp.concatenate([imag_hi, -real_hi] * 4 + [imag_lo, -real_lo] * 4, axis=0)
        weights.append((first, second))
    for part, (low, high) in enumerate(EIG_PARTS):
        eig_copies[part].wait()
        for k in range(low, high):
            first, second = weights[k]
            real_hi, real_lo = split(eig[0, k])
            imag_hi, imag_lo = split(eig[1, k])
            both = dot_t(jnp.concatenate([real_hi, real_lo], axis=0), first)
            both = both + dot_t(jnp.concatenate([imag_hi, imag_lo], axis=0), second)
            series[k, :DOF, :] = (both[:DOF, :128] + both[:DOF, 128:]) + both[DOF:, :128]
        for k in range(low, high):
            for chunk in range(4):
                message = None
                for i in range(QUAD):
                    rows = series[k, pl.ds(chunk * PER_DEV + i, 16, stride=QUAD), :]
                    message = rows if message is None else jnp.where(lane_quad == i, rows, message)
                out_ref[(4 * k + chunk) * 16 : (4 * k + chunk + 1) * 16, :] = message


def project(velocities, mass_root, eigvec, q_points, cell_offsets):
    return pl.pallas_call(
        project_kernel,
        out_shape=jax.ShapeDtypeStruct((512, 128), F32),
        in_specs=[pl.BlockSpec(memory_space=pltpu.HBM)] * 5,
        out_specs=pl.BlockSpec(memory_space=pltpu.VMEM),
        scratch_shapes=[
            pltpu.SMEM((3, QPTS), jnp.int32),
            pltpu.VMEM((3, CELLS), jnp.int32),
            pltpu.VMEM((1, DOF), F32),
            pltpu.VMEM((FRAMES, DOF, CELLS), BF16),
            pltpu.VMEM((2, QPTS, DOF, DOF), F32),
            pltpu.VMEM((2, 256, 128), F32),
            pltpu.VMEM((QPTS, DOF + 8, 128), F32),
            pltpu.SemaphoreType.DMA((3,)),
            pltpu.SemaphoreType.DMA((VEL_PARTS,)),
            pltpu.SemaphoreType.DMA((len(EIG_PARTS),)),
        ],
        compiler_params=pltpu.CompilerParams(vmem_limit_bytes=32 * 1024 * 1024),
        name="project",
    )(
        *[
            pltpu.with_memory_space_constraint(operand, pltpu.HBM)
            for operand in (q_points, cell_offsets, mass_root.reshape(1, DOF), velocities, eigvec)
        ]
    )


def transform_kernel(x_ref, low_ref, twist_ref, dft_ref, turn_ref, out_ref):
    block = lax.broadcasted_iota(jnp.int32, (16, 128), 1) // 4
    rows = [x_ref[d * 16 : (d + 1) * 16, :] for d in range(32)]
    rows = [pltpu.roll(row, 4 * d, 1) if d else row for d, row in enumerate(rows)]
    for bit in (1, 2, 4, 8, 16):
        moves = (block & bit) != 0
        rows = [jnp.where(moves, rows[(d + bit) % 32], rows[d]) for d in range(32)]
    rows = [rows[-n % 32] for n in range(32)]
    rows = [pltpu.roll(row, 128 - 4 * n, 1) if n else row for n, row in enumerate(rows)]
    low_hi = jnp.concatenate([low_ref[0]] * 2, axis=1)
    parts = []
    for residue in range(4):
        gathered = jnp.concatenate(rows[residue::4], axis=0)
        hi, lo = split(gathered)
        low = dot(low_hi, jnp.concatenate([hi, lo], axis=0)) + dot(low_ref[1], hi)
        real, imag = low[:64], low[64:]
        cosine, sine = [
            jnp.concatenate([twist_ref[2 * residue + part]] * QUAD, axis=0) for part in range(2)
        ]
        parts += [real * cosine + imag * sine, imag * cosine - real * sine]
    hi, lo = split(jnp.concatenate(parts, axis=0))
    both = dot(jnp.concatenate([hi, lo], axis=1), jnp.concatenate([dft_ref[0]] * 2, axis=0))
    both = both + dot(hi, dft_ref[1])
    real, imag = [], []
    for residue in range(4):
        upper = both[residue * 128 : residue * 128 + 64]
        lower = both[residue * 128 + 64 : residue * 128 + 128]
        a = upper[:, :128] + lower[:, 128:]
        b = lower[:, :128] - upper[:, 128:]
        if residue:
            cosine = turn_ref[2 * residue : 2 * residue + 1, :]
            sine = turn_ref[2 * residue + 1 : 2 * residue + 2, :]
            a, b = a * cosine + b * sine, b * cosine - a * sine
        real.append(a)
        imag.append(b)
    sum_real, sum_imag = real[0] + real[2], imag[0] + imag[2]
    gap_real, gap_imag = real[0] - real[2], imag[0] - imag[2]
    odd_real, odd_imag = real[1] + real[3], imag[1] + imag[3]
    far_real, far_imag = real[1] - real[3], imag[1] - imag[3]
    quarters = [
        (sum_real + odd_real, sum_imag + odd_imag),
        (gap_real + far_imag, gap_imag - far_real),
        (sum_real - odd_real, sum_imag - odd_imag),
        (gap_real - far_imag, gap_imag + far_real),
    ]
    for j, (a, b) in enumerate(quarters):
        power = (a * a + b * b) * (1.0 / TOTAL)
        for i in range(QUAD):
            out_ref[pl.ds(i * 4 + j, 16, stride=16), :] = power[i * 16 : (i + 1) * 16, :]


def split_np(x):
    hi = x.astype(np.float32).astype(jnp.bfloat16)
    lo = (x - hi.astype(np.float64)).astype(np.float32).astype(jnp.bfloat16)
    return hi, lo


@functools.cache
def tables():
    g = np.arange(16)
    theta = 2.0 * np.pi * (g[:, None] * g[None, :] % 16) / 16
    theta = theta[GROUPS][:, GROUPS]
    low = np.zeros((2, QUAD, 16, QUAD, 2, 16))
    for i in range(QUAD):
        low[0, i, :, i, 0] = np.cos(theta)
        low[0, i, :, i, 1] = np.sin(theta)
        low[1, i, :, i, 0] = -np.sin(theta)
        low[1, i, :, i, 1] = np.cos(theta)
    hi, lo = split_np(low.reshape(128, 128))
    low = np.stack([hi, lo])
    n = np.arange(SPAN // 4)
    residue = np.arange(4)
    s = 4 * n[None, :] + residue[:, None]
    twist = 2.0 * np.pi * GROUPS[:, None] * s[:, None, :] / TOTAL
    twist = np.stack([np.cos(twist), np.sin(twist)], axis=1).reshape(8, 16, SPAN // 4)
    full = 2.0 * np.pi * (n[:, None] * n[None, :] % 128) / 128
    hi, lo = split_np(np.concatenate([np.cos(full), np.sin(full)], axis=1))
    dft = np.stack([hi, lo])
    turn = 2.0 * np.pi * residue[:, None] * n / SPAN
    turn = np.stack([np.cos(turn), np.sin(turn)], axis=1).reshape(8, SPAN // 4)
    return low, twist.astype(np.float32), dft, turn.astype(np.float32)


def transform(x):
    return pl.pallas_call(
        transform_kernel,
        out_shape=jax.ShapeDtypeStruct((256, 128), F32),
        in_specs=[pl.BlockSpec(memory_space=pltpu.VMEM)] * 5,
        out_specs=pl.BlockSpec(memory_space=pltpu.VMEM),
        compiler_params=pltpu.CompilerParams(vmem_limit_bytes=32 * 1024 * 1024),
        name="transform",
    )(x, *[jnp.asarray(table) for table in tables()])


def per_device(velocities, mass_root, eigvec, q_points, cell_offsets):
    messages = project(velocities, mass_root, eigvec, q_points, cell_offsets)
    frames = lax.all_to_all(
        messages.reshape(512, 1, 128), ("dev", "grp_high", "grp_x", "grp_low"), 0, 0, tiled=True
    )
    power = transform(frames.reshape(512, 128))
    spectra = lax.all_to_all(
        power.reshape(16, 16, 128), ("grp_high", "grp_x", "grp_low"), 0, 0, tiled=True
    )
    rows = spectra.reshape(256, 128)[: PER_DEV * 4]
    return rows.reshape(1, PER_DEV, SPAN)


def solution(mesh):
    grp = ("grp_high", "grp_low", "grp_x")
    split_mesh = Mesh(mesh.devices.reshape(2, 4, 2, N_DEV), grp + ("dev",))
    return jax.shard_map(
        per_device,
        mesh=split_mesh,
        in_specs=(P(grp + ("dev",), None, None), P(), P(), P(), P()),
        out_specs=P(grp, "dev", None),
        check_vma=False,
    )
```

```python
import functools
import math

import jax
import jax.numpy as jnp
import numpy as np
from jax import lax
from jax.experimental import pallas as pl
from jax.experimental.pallas import tpu as pltpu
from jax.sharding import Mesh
from jax.sharding import PartitionSpec as P

LAT = 8
CELLS = 512
DOF = 240
QPTS = 8
TOTAL = 8192
N_GRP = 16
N_DEV = 32
FRAMES = 16
PER_DEV = 60
QUAD = 4
SPAN = 512
GROUPS = np.arange(N_GRP).reshape(2, 4, 2).transpose(0, 2, 1).ravel()
VEL_PARTS = 2
EIG_PARTS = ((0, 4), (4, 8))
EIG_STARTS = ((0,), (1,), ())
F32 = jnp.float32
BF16 = jnp.bfloat16


def split(x):
    hi = x.astype(BF16)
    return hi, (x - hi.astype(F32)).astype(BF16)


def dot_t(a, b):
    return lax.dot_general(a, b, (((1,), (1,)), ((), ())), preferred_element_type=F32)


def dot(a, b):
    return jnp.dot(a, b, preferred_element_type=F32)


def cosine_of(eighths):
    one = CELLS**-0.5
    half = math.sqrt(0.5) * CELLS**-0.5
    near = jnp.where((eighths == 1) | (eighths == 7), half, 0.0)
    far = jnp.where((eighths == 3) | (eighths == 5), -half, near)
    return jnp.where(eighths == 0, one, jnp.where(eighths == 4, -one, far))


def project_kernel(
    q_hbm, cell_hbm, mass_hbm, vel_hbm, eig_hbm, out_ref,
    q_ref, cell_ref, mass_ref, vel, eig, summed, series, small_sem, vel_sem, eig_sem,
):
    small_copies = [
        pltpu.make_async_copy(source, target, small_sem.at[n])
        for n, (source, target) in enumerate(
            [(q_hbm, q_ref), (cell_hbm, cell_ref), (mass_hbm, mass_ref)]
        )
    ]
    for copy in small_copies:
        copy.start()
    vel_copies = []
    for part in range(VEL_PARTS):
        frames = pl.ds(part * FRAMES // VEL_PARTS, FRAMES // VEL_PARTS)
        copy = pltpu.make_async_copy(vel_hbm.at[frames], vel.at[frames], vel_sem.at[part])
        copy.start()
        vel_copies.append(copy)
    eig_copies = []
    for part, (low, high) in enumerate(EIG_PARTS):
        ks = pl.ds(low, high - low)
        eig_copies.append(pltpu.make_async_copy(eig_hbm.at[:, ks], eig.at[:, ks], eig_sem.at[part]))
    for part in EIG_STARTS[0]:
        eig_copies[part].start()

    for copy in small_copies:
        copy.wait()
    row = lax.broadcasted_iota(jnp.int32, (QPTS, CELLS), 0)
    products = jnp.zeros((QPTS, CELLS), jnp.int32)
    for j in range(3):
        column = jnp.zeros((QPTS, CELLS), jnp.int32)
        for k in range(QPTS):
            column = jnp.where(row == k, q_ref[j, k], column)
        products = products + column * cell_ref[j : j + 1, :]
    eighths = products & (LAT - 1)
    phases = jnp.concatenate(
        [cosine_of(eighths), cosine_of((eighths + 6) & (LAT - 1))], axis=0
    ).astype(BF16)

    mass = mass_ref[...]
    for t in range(FRAMES):
        if t % (FRAMES // VEL_PARTS) == 0:
            vel_copies[t // (FRAMES // VEL_PARTS)].wait()
            for part in EIG_STARTS[1 + t // (FRAMES // VEL_PARTS)]:
                eig_copies[part].start()
        sums = dot_t(phases, vel[t]) * mass
        at = (t % 4 * 4 + t // 4) * 16
        summed[0, at : at + 16, :] = sums[:, :128]
        summed[1, at : at + 16, : DOF - 128] = sums[:, 128:]

    series[:, DOF:, :] = jnp.zeros((QPTS, 8, 128), F32)
    lane_quad = lax.broadcasted_iota(jnp.int32, (16, 128), 1) // 32
    weights = []
    for k in range(QPTS):
        real, imag = [
            jnp.concatenate(
                [summed[lanes, pl.ds(start, 16, stride=16), :] for lanes in range(2)], axis=1
            )[:, :DOF]
            for start in (k, 8 + k)
        ]
        (real_hi, real_lo), (imag_hi, imag_lo) = split(real), split(imag)
        first = jnp.concatenate([real_hi, imag_hi] * 4 + [real_lo, imag_lo] * 4, axis=0)
        second = jnp.concatenate([imag_hi, -real_hi] * 4 + [imag_lo, -real_lo] * 4, axis=0)
        weights.append((first, second))
    for part, (low, high) in enumerate(EIG_PARTS):
        eig_copies[part].wait()
        for k in range(low, high):
            first, second = weights[k]
            real_hi, real_lo = split(eig[0, k])
            imag_hi, imag_lo = split(eig[1, k])
            both = dot_t(jnp.concatenate([real_hi, real_lo], axis=0), first)
            both = both + dot_t(jnp.concatenate([imag_hi, imag_lo], axis=0), second)
            series[k, :DOF, :] = both[:DOF, :128] + (both[:DOF, 128:] + both[DOF:, :128])
        for k in range(low, high):
            for chunk in range(4):
                message = None
                for i in range(QUAD):
                    rows = series[k, pl.ds(chunk * PER_DEV + i, 16, stride=QUAD), :]
                    message = rows if message is None else jnp.where(lane_quad == i, rows, message)
                out_ref[(4 * k + chunk) * 16 : (4 * k + chunk + 1) * 16, :] = message


def project(velocities, mass_root, eigvec, q_points, cell_offsets):
    return pl.pallas_call(
        project_kernel,
        out_shape=jax.ShapeDtypeStruct((512, 128), F32),
        in_specs=[pl.BlockSpec(memory_space=pltpu.HBM)] * 5,
        out_specs=pl.BlockSpec(memory_space=pltpu.VMEM),
        scratch_shapes=[
            pltpu.SMEM((3, QPTS), jnp.int32),
            pltpu.VMEM((3, CELLS), jnp.int32),
            pltpu.VMEM((1, DOF), F32),
            pltpu.VMEM((FRAMES, DOF, CELLS), BF16),
            pltpu.VMEM((2, QPTS, DOF, DOF), F32),
            pltpu.VMEM((2, 256, 128), F32),
            pltpu.VMEM((QPTS, DOF + 8, 128), F32),
            pltpu.SemaphoreType.DMA((3,)),
            pltpu.SemaphoreType.DMA((VEL_PARTS,)),
            pltpu.SemaphoreType.DMA((len(EIG_PARTS),)),
        ],
        compiler_params=pltpu.CompilerParams(vmem_limit_bytes=32 * 1024 * 1024),
        name="project",
    )(
        *[
            pltpu.with_memory_space_constraint(operand, pltpu.HBM)
            for operand in (q_points, cell_offsets, mass_root.reshape(1, DOF), velocities, eigvec)
        ]
    )


def transform_kernel(x_ref, low_ref, twist_ref, dft_ref, turn_ref, out_ref):
    block = lax.broadcasted_iota(jnp.int32, (16, 128), 1) // 4
    rows = [x_ref[d * 16 : (d + 1) * 16, :] for d in range(32)]
    rows = [pltpu.roll(row, 4 * d, 1) if d else row for d, row in enumerate(rows)]
    for bit in (1, 2, 4, 8, 16):
        moves = (block & bit) != 0
        rows = [jnp.where(moves, rows[(d + bit) % 32], rows[d]) for d in range(32)]
    rows = [rows[-n % 32] for n in range(32)]
    rows = [pltpu.roll(row, 128 - 4 * n, 1) if n else row for n, row in enumerate(rows)]
    low_hi = jnp.concatenate([low_ref[0]] * 2, axis=1)
    parts = []
    for residue in range(4):
        gathered = jnp.concatenate(rows[residue::4], axis=0)
        hi, lo = split(gathered)
        low = dot(low_hi, jnp.concatenate([hi, lo], axis=0)) + dot(low_ref[1], hi)
        real, imag = low[:64], low[64:]
        cosine, sine = [
            jnp.concatenate([twist_ref[2 * residue + part]] * QUAD, axis=0) for part in range(2)
        ]
        parts += [real * cosine + imag * sine, imag * cosine - real * sine]
    hi, lo = split(jnp.concatenate(parts, axis=0))
    both = dot(jnp.concatenate([hi, lo], axis=1), jnp.concatenate([dft_ref[0]] * 2, axis=0))
    both = both + dot(hi, dft_ref[1])
    real, imag = [], []
    for residue in range(4):
        upper = both[residue * 128 : residue * 128 + 64]
        lower = both[residue * 128 + 64 : residue * 128 + 128]
        a = upper[:, :128] + lower[:, 128:]
        b = lower[:, :128] - upper[:, 128:]
        if residue:
            cosine = turn_ref[2 * residue : 2 * residue + 1, :]
            sine = turn_ref[2 * residue + 1 : 2 * residue + 2, :]
            a, b = a * cosine + b * sine, b * cosine - a * sine
        real.append(a)
        imag.append(b)
    sum_real, sum_imag = real[0] + real[2], imag[0] + imag[2]
    gap_real, gap_imag = real[0] - real[2], imag[0] - imag[2]
    odd_real, odd_imag = real[1] + real[3], imag[1] + imag[3]
    far_real, far_imag = real[1] - real[3], imag[1] - imag[3]
    quarters = [
        (sum_real + odd_real, sum_imag + odd_imag),
        (gap_real + far_imag, gap_imag - far_real),
        (sum_real - odd_real, sum_imag - odd_imag),
        (gap_real - far_imag, gap_imag + far_real),
    ]
    for j, (a, b) in enumerate(quarters):
        power = (a * a + b * b) * (1.0 / TOTAL)
        for i in range(QUAD):
            out_ref[pl.ds(i * 4 + j, 16, stride=16), :] = power[i * 16 : (i + 1) * 16, :]


def split_np(x):
    hi = x.astype(np.float32).astype(jnp.bfloat16)
    lo = (x - hi.astype(np.float64)).astype(np.float32).astype(jnp.bfloat16)
    return hi, lo


@functools.cache
def tables():
    g = np.arange(16)
    theta = 2.0 * np.pi * (g[:, None] * g[None, :] % 16) / 16
    theta = theta[GROUPS][:, GROUPS]
    low = np.zeros((2, QUAD, 16, QUAD, 2, 16))
    for i in range(QUAD):
        low[0, i, :, i, 0] = np.cos(theta)
        low[0, i, :, i, 1] = np.sin(theta)
        low[1, i, :, i, 0] = -np.sin(theta)
        low[1, i, :, i, 1] = np.cos(theta)
    hi, lo = split_np(low.reshape(128, 128))
    low = np.stack([hi, lo])
    n = np.arange(SPAN // 4)
    residue = np.arange(4)
    s = 4 * n[None, :] + residue[:, None]
    twist = 2.0 * np.pi * GROUPS[:, None] * s[:, None, :] / TOTAL
    twist = np.stack([np.cos(twist), np.sin(twist)], axis=1).reshape(8, 16, SPAN // 4)
    full = 2.0 * np.pi * (n[:, None] * n[None, :] % 128) / 128
    hi, lo = split_np(np.concatenate([np.cos(full), np.sin(full)], axis=1))
    dft = np.stack([hi, lo])
    turn = 2.0 * np.pi * residue[:, None] * n / SPAN
    turn = np.stack([np.cos(turn), np.sin(turn)], axis=1).reshape(8, SPAN // 4)
    return low, twist.astype(np.float32), dft, turn.astype(np.float32)


def transform(x):
    return pl.pallas_call(
        transform_kernel,
        out_shape=jax.ShapeDtypeStruct((256, 128), F32),
        in_specs=[pl.BlockSpec(memory_space=pltpu.VMEM)] * 5,
        out_specs=pl.BlockSpec(memory_space=pltpu.VMEM),
        compiler_params=pltpu.CompilerParams(vmem_limit_bytes=32 * 1024 * 1024),
        name="transform",
    )(x, *[jnp.asarray(table) for table in tables()])


def per_device(velocities, mass_root, eigvec, q_points, cell_offsets):
    messages = project(velocities, mass_root, eigvec, q_points, cell_offsets)
    frames = lax.all_to_all(
        messages.reshape(512, 1, 128), ("dev", "grp_high", "grp_x", "grp_low"), 0, 0, tiled=True
    )
    power = transform(frames.reshape(512, 128))
    spectra = lax.all_to_all(
        power.reshape(16, 16, 128), ("grp_high", "grp_x", "grp_low"), 0, 0, tiled=True
    )
    rows = spectra.reshape(256, 128)[: PER_DEV * 4]
    return rows.reshape(1, PER_DEV, SPAN)


def solution(mesh):
    grp = ("grp_high", "grp_low", "grp_x")
    split_mesh = Mesh(mesh.devices.reshape(2, 4, 2, N_DEV), grp + ("dev",))
    return jax.shard_map(
        per_device,
        mesh=split_mesh,
        in_specs=(P(grp + ("dev",), None, None), P(), P(), P(), P()),
        out_specs=P(grp, "dev", None),
        check_vma=False,
    )
```
